32 devices in a mesh: groups: 2 (over x), tok: 16 (over z, y, core).
Axes of the slice: x: 2, y: 2, z: 4, core: 2. Of those that a mesh axis runs over, the one named last changes fastest.
Arguments:
- tokens: bfloat16 [4, 8192, 512], P('groups', 'tok'), parts along dimension 0, may hold values from -28 to 28
- w_query: bfloat16 [512, 512], replicated, may hold values from -0.25 to 0.25
- w_key: bfloat16 [512, 512], replicated, may hold values from -0.25 to 0.25
- w_value: bfloat16 [512, 512], replicated, may hold values from -0.25 to 0.25
- w_out: bfloat16 [512, 512], replicated, may hold values from -0.25 to 0.25
- partner_block: int32 [16, 4], P('tok'), may hold values from 0 to 3
- head_masks: int32 [16, 4, 8], P('tok'), may hold values 0 or 1
- cotangent: bfloat16 [4, 8192, 512], P('groups', 'tok'), parts along dimension 0, may hold values from -6 to 6
Outputs:
- output: bfloat16 [4, 8192, 512], P('groups', 'tok'), parts along dimension 0
- grad_tokens: bfloat16 [4, 8192, 512], P('groups', 'tok'), parts along dimension 0
- grad_query: float32 [1024, 512], P('groups'), parts along dimension 0
- grad_key: float32 [1024, 512], P('groups'), parts along dimension 0
- grad_value: float32 [1024, 512], P('groups'), parts along dimension 0
- grad_out: float32 [1024, 512], P('groups'), parts along dimension 0
The draws below stay inside these ranges and needn't reach their ends.
There are 2 independent parts, one for each index of `groups`. The reference program is written for one: setup_inputs(seed, part) draws one part's arguments, and reference() takes and returns one part's arrays. A program takes and returns all parts, laid end to end along the dimension named above; an argument that names none is the same for every part. Nothing has to cross between parts.
All inputs are finite; a program needn't handle non-finite values. No bound on the sum of `head_masks` on one device may be relied on, other than what follows from the above.
Results may differ from the reference program's by a relative error of at most 0.015.
The reference program's roundings to bfloat16 on the way count: a program that leaves them out, or rounds other values in their place, can miss the bound.
Values may be sent and summed in bfloat16 or wider, within the bound.
No kernel may reach another device: no remote copies, remote signals or barrier semaphores. Data moves between devices by JAX's collectives and lax.ppermute only.
A program may use at most 128 MiB of HBM per device.

```python
import math
import jax
import jax.numpy as jnp
from jax import lax

SAMPLES = 2
BLOCK = 512
SUB = 128
D = 512
HEADS = 8
HDIM = 64
TOKENS = 8192
N_TOK = 16


def draw_tokens(key, part):
    shape = (SAMPLES, TOKENS, D)
    return jnp.clip(jax.random.normal(key, shape, jnp.float32), -4.0, 4.0).astype(jnp.bfloat16)


def touch_ends(values, key, smallest, top_value):
    index_at = [jax.random.randint(jax.random.fold_in(key, axis), (), 0, length) for axis, length in enumerate(values.shape)]
    longest = values.shape.index(max(values.shape))
    next_to = index_at[:longest] + [(index_at[longest] + 1) % values.shape[longest]] + index_at[longest + 1:]
    return values.at[tuple(index_at)].set(smallest).at[tuple(next_to)].set(top_value)


def block_levels(own_key, shape, cuts, low, high):
    def one(dim, blocks):
        heights = jax.random.uniform(jax.random.fold_in(jax.random.fold_in(own_key, 6), dim), (blocks,), jnp.float32, low / len(cuts), high / len(cuts))
        return jnp.repeat(jnp.exp(heights), shape[dim] // blocks).reshape((-1,) + (1,) * (len(shape) - dim - 1))

    factor_of = one(*cuts[0])
    for cut in cuts[1:]:
        factor_of = factor_of * one(*cut)
    return factor_of


def noise(key, dims, spread, reach, cuts=(), kind=jnp.bfloat16):
    array = jax.random.normal(key, dims, jnp.float32) * spread
    if len(cuts) > 0:
        array = block_levels(key, dims, cuts, -0.22, 0.18) * array
    return jnp.clip(array, min=-reach, max=reach).astype(kind)


def setup_inputs(seed: int = 0, part: int = 0) -> dict:
    key_list = jax.random.split(jax.random.key(seed), 9)
    part_keys = jax.random.split(jax.random.fold_in(key_list[8], part), 9)
    tokens = draw_tokens(jax.random.fold_in(jax.random.fold_in(key_list[8], part), 71), part)
    w_query = noise(key_list[1], (D, D), D ** -0.5, 0.25)
    w_key = noise(key_list[2], (D, D), D ** -0.5, 0.25)
    w_value = noise(key_list[3], (D, D), D ** -0.5, 0.25)
    w_out = noise(key_list[4], (D, D), D ** -0.5, 0.25)
    partner_block = touch_ends(jax.random.randint(key_list[5], (N_TOK, 4), 0, BLOCK // SUB), jax.random.fold_in(key_list[5], 1), 0, (BLOCK // SUB) - 1).astype(jnp.int32)
    head_masks = touch_ends((jax.random.randint(key_list[6], (N_TOK, 4, HEADS), 0, 4) < 3).astype(jnp.int32), jax.random.fold_in(key_list[6], 1), 0, 1)
    cotangent = noise(part_keys[7], (SAMPLES, TOKENS, D), 1.0, 6.0, ((1, 16),))
    return dict(tokens=tokens, w_query=w_query, w_key=w_key, w_value=w_value, w_out=w_out, partner_block=partner_block, head_masks=head_masks, cotangent=cotangent)


def attend(queries, gathered, mask_rows, grad_output, w_out, score_scale):
    samples, block_rows, model_width = queries.shape
    head_count = mask_rows.shape[1]
    head_width = model_width // head_count
    key_count = gathered.shape[1]
    sub_rows = (key_count - block_rows) // 4
    f32 = jnp.float32
    query_heads = queries.reshape(samples, block_rows, head_count, head_width).astype(f32)
    key_heads = gathered[..., :model_width].reshape(samples, key_count, head_count, head_width).astype(f32)
    value_heads = gathered[..., model_width:].reshape(samples, key_count, head_count, head_width).astype(f32)
    visible = jnp.concatenate([jnp.ones((head_count, block_rows), jnp.int32), jnp.repeat(mask_rows.T, sub_rows, axis=1)], 1) > 0
    scores = jnp.einsum('sqhd,skhd->shqk', query_heads, key_heads) * score_scale
    scores = jnp.where(visible[None, :, None, :], scores, -jnp.inf)
    row_max = lax.optimization_barrier(jnp.max(scores, axis=-1, keepdims=True))
    expo_terms = jnp.exp(scores - row_max)
    probability = expo_terms / lax.optimization_barrier(jnp.sum(expo_terms, axis=-1, keepdims=True))
    prob_half = probability.astype(jnp.bfloat16)
    context = jnp.einsum('shqk,skhd->sqhd', prob_half.astype(f32), value_heads).astype(jnp.bfloat16)
    context_rows = context.reshape(samples * block_rows, model_width)
    output = jnp.dot(context_rows, w_out, preferred_element_type=f32).astype(jnp.bfloat16)
    grad_rows = grad_output.reshape(samples * block_rows, model_width)
    grad_context = jnp.dot(grad_rows, w_out.T, preferred_element_type=f32).astype(jnp.bfloat16)
    grad_context = grad_context.reshape(samples, block_rows, head_count, head_width)
    grad_prob = jnp.einsum('sqhd,skhd->shqk', grad_context.astype(f32), value_heads)
    row_dot = lax.optimization_barrier(jnp.sum(grad_context.astype(f32) * context.astype(f32), axis=-1)).transpose(0, 2, 1)
    grad_score = (probability * (grad_prob - row_dot[..., None]) * score_scale).astype(jnp.bfloat16)
    grad_q = jnp.einsum('shqk,skhd->sqhd', grad_score.astype(f32), key_heads).astype(jnp.bfloat16)
    grad_k = jnp.einsum('shqk,sqhd->skhd', grad_score.astype(f32), query_heads)
    grad_v = jnp.einsum('shqk,sqhd->skhd', prob_half.astype(f32), grad_context.astype(f32))
    key_grads = jnp.concatenate([grad_k.reshape(samples, key_count, model_width), grad_v.reshape(samples, key_count, model_width)], -1)
    return (output.reshape(samples, block_rows, model_width), context_rows.reshape(samples, block_rows, model_width), grad_q.reshape(samples, block_rows, model_width), key_grads)

def reference(tokens, w_query, w_key, w_value, w_out, partner_block, head_masks, cotangent):
    f32 = jnp.float32
    score_scale = 1.0 / math.sqrt(HDIM)
    levels = N_TOK.bit_length() - 1
    token_rows = tokens.reshape(SAMPLES * TOKENS, D)
    queries = jnp.dot(token_rows, w_query, preferred_element_type=f32).astype(jnp.bfloat16).reshape(SAMPLES, TOKENS, D)
    w_key_value = jnp.concatenate([w_key, w_value], 1)
    key_value = jnp.dot(token_rows, w_key_value, preferred_element_type=f32).astype(jnp.bfloat16).reshape(SAMPLES, TOKENS, 2 * D)

    def one_block(key_grads, block_index):
        first_row = (block_index * BLOCK).astype(jnp.int32)
        window_queries = lax.dynamic_slice_in_dim(queries, first_row, BLOCK, 1)
        pieces = [lax.dynamic_slice_in_dim(key_value, first_row, BLOCK, 1)]
        starts = [first_row]
        for section in range(4):
            partner_dev = jnp.bitwise_xor(block_index, 1 << levels - 4 + section)
            start_row = (partner_dev * BLOCK + partner_block[block_index, section] * SUB).astype(jnp.int32)
            pieces.append(lax.dynamic_slice_in_dim(key_value, start_row, SUB, 1))
            starts.append(start_row)
        gathered = jnp.concatenate(pieces, 1)
        grad_output = lax.dynamic_slice_in_dim(cotangent, first_row, BLOCK, 1)
        output, context, grad_q, block_grads = attend(window_queries, gathered, head_masks[block_index], grad_output, w_out, score_scale)
        offset = 0
        for start_row, row_count in zip(starts, [BLOCK, SUB, SUB, SUB, SUB]):
            addend = block_grads[:, offset:offset + row_count]
            current = lax.dynamic_slice_in_dim(key_grads, start_row, row_count, 1)
            key_grads = lax.dynamic_update_slice_in_dim(key_grads, current + addend, start_row, 1)
            offset += row_count
        return (key_grads, (output, context, grad_q))
    initial = jnp.zeros((SAMPLES, TOKENS, 2 * D), f32)
    key_grads, (outputs, contexts, grad_qs) = lax.scan(one_block, initial, jnp.arange(N_TOK, dtype=jnp.int32))

    def merge_blocks(stacked):
        return stacked.transpose(1, 0, 2, 3).reshape(SAMPLES * TOKENS, D)
    output = merge_blocks(outputs).reshape(SAMPLES, TOKENS, D)
    context_rows = merge_blocks(contexts)
    grad_q_rows = merge_blocks(grad_qs)
    grad_kv_rows = key_grads.astype(jnp.bfloat16).reshape(SAMPLES * TOKENS, 2 * D)
    grad_tokens = (jnp.dot(grad_q_rows, w_query.T, preferred_element_type=f32) + jnp.dot(grad_kv_rows, w_key_value.T, preferred_element_type=f32)).astype(jnp.bfloat16)
    grad_query = jnp.dot(token_rows.T, grad_q_rows, preferred_element_type=f32)
    grad_pair = jnp.dot(token_rows.T, grad_kv_rows, preferred_element_type=f32)
    grad_out = jnp.dot(context_rows.T, cotangent.reshape(SAMPLES * TOKENS, D), preferred_element_type=f32)
    return (output, grad_tokens.reshape(SAMPLES, TOKENS, D), grad_query, grad_pair[:, :D], grad_pair[:, D:], grad_out)
```

```python
import functools

import jax
import jax.numpy as jnp
from jax import lax
from jax.experimental import pallas as pl
from jax.experimental.pallas import tpu as pltpu
from jax.sharding import PartitionSpec as P

SUB = 128
GROUPS = 1
VMEM = 48 * 1024 * 1024
F32 = jnp.float32
BF16 = jnp.bfloat16
OFF = 1e30


def partner(x, stride):
    return lax.ppermute(x, "tok", [(i, i ^ 1 << stride) for i in range(lax.axis_size("tok"))])


def nn(a, b):
    return lax.dot_general(a, b, (((1,), (0,)), ((), ())), preferred_element_type=F32)


def nt(a, b):
    return lax.dot_general(a, b, (((1,), (1,)), ((), ())), preferred_element_type=F32)


def tn(a, b):
    return lax.dot_general(a, b, (((0,), (0,)), ((), ())), preferred_element_type=F32)


def tt(a, b):
    return lax.dot_general(a, b, (((0,), (1,)), ((), ())), preferred_element_type=F32)


def params(*semantics):
    return pltpu.CompilerParams(vmem_limit_bytes=VMEM, dimension_semantics=semantics or None)


def head_rows(pair_rows, which, head_width):
    row = lax.broadcasted_iota(jnp.int32, pair_rows.shape, 0)
    keep = (row >= which * head_width) & (row < (which + 1) * head_width)
    return jnp.where(keep, pair_rows, jnp.zeros_like(pair_rows))


def project_kernel(scale, x_ref, c_ref, wq_ref, wk_ref, wv_ref, wo_ref, qt_ref, k_ref, v_ref, kt_ref, vt_ref, dot_ref):
    x = x_ref[0]
    qt_ref[0] = (tt(wq_ref[...], x).astype(BF16).astype(F32) * scale).astype(BF16)
    k = nn(x, wk_ref[...])
    v = nn(x, wv_ref[...])
    k_ref[0] = k.astype(BF16)
    v_ref[0] = v.astype(BF16)
    kt_ref[0] = k.T.astype(BF16)
    vt_ref[0] = v.T.astype(BF16)
    dot_ref[0] = nt(wo_ref[...], c_ref[0]).astype(BF16)


def project(tokens, cotangent, w_query, w_key, w_value, w_out, scale):
    samples, rows, width = tokens.shape
    row_block = pl.BlockSpec((1, rows, width), lambda s: (s, 0, 0))
    col_block = pl.BlockSpec((1, width, rows), lambda s: (s, 0, 0))
    whole = pl.BlockSpec((width, width), lambda s: (0, 0))
    by_row = jax.ShapeDtypeStruct((samples, rows, width), BF16)
    by_col = jax.ShapeDtypeStruct((samples, width, rows), BF16)
    return pl.pallas_call(
        functools.partial(project_kernel, scale),
        grid=(samples,),
        in_specs=[row_block, row_block] + [whole] * 4,
        out_specs=[col_block, row_block, row_block, col_block, col_block, col_block],
        out_shape=[by_col, by_row, by_row, by_col, by_col, by_col],
        compiler_params=params("arbitrary"),
    )(tokens, cotangent, w_query, w_key, w_value, w_out)


def project_partner_kernel(x0, x1, x2, x3, wk_ref, wv_ref, k_ref, v_ref, kt_ref, vt_ref):
    x = jnp.concatenate([x0[0], x1[0], x2[0], x3[0]], 0)
    k = nn(x, wk_ref[...])
    v = nn(x, wv_ref[...])
    k_ref[0] = k.astype(BF16)
    v_ref[0] = v.astype(BF16)
    kt_ref[0] = k.T.astype(BF16)
    vt_ref[0] = v.T.astype(BF16)


def project_partner(arrived, w_key, w_value):
    samples, sub_rows, width = arrived[0].shape
    rows = sub_rows * len(arrived)
    part = pl.BlockSpec((1, sub_rows, width), lambda s: (s, 0, 0))
    row_block = pl.BlockSpec((1, rows, width), lambda s: (s, 0, 0))
    col_block = pl.BlockSpec((1, width, rows), lambda s: (s, 0, 0))
    whole = pl.BlockSpec((width, width), lambda s: (0, 0))
    by_row = jax.ShapeDtypeStruct((samples, rows, width), BF16)
    by_col = jax.ShapeDtypeStruct((samples, width, rows), BF16)
    return pl.pallas_call(
        project_partner_kernel,
        grid=(samples,),
        in_specs=[part] * 4 + [whole] * 2,
        out_specs=[row_block, row_block, col_block, col_block],
        out_shape=[by_row, by_row, by_col, by_col],
        compiler_params=params("arbitrary"),
    )(*arrived, w_key, w_value)


def own_kernel(head_width, qt_ref, k_ref, vt_ref, e_ref, o_ref, st_ref):
    k = k_ref[0]
    for which in range(2):
        s = nn(k, head_rows(qt_ref[0], which, head_width))
        top = jnp.max(s, axis=0, keepdims=True)
        e = jnp.exp(s - top)
        total = jnp.sum(e, axis=0, keepdims=True)
        e = e.astype(BF16)
        e_ref[0, which] = e
        o_ref[0, which] = nn(vt_ref[0, which * head_width : (which + 1) * head_width, :], e)
        st_ref[0, which] = jnp.concatenate([top, total, jnp.zeros((6, top.shape[1]), F32)], 0)


def own_part(qt, k, vt, head_count):
    samples, width, rows = qt.shape
    head_width = width // head_count
    col_pair = pl.BlockSpec((1, 2 * head_width, rows), lambda p, s: (s, p, 0))
    row_pair = pl.BlockSpec((1, rows, 2 * head_width), lambda p, s: (s, 0, p))

    def per_head(n):
        return pl.BlockSpec((1, 2, n, rows), lambda p, s: (s, p, 0, 0))

    return pl.pallas_call(
        functools.partial(own_kernel, head_width),
        grid=(head_count // 2, samples),
        in_specs=[col_pair, row_pair, col_pair],
        out_specs=[per_head(rows), per_head(head_width), per_head(8)],
        out_shape=[
            jax.ShapeDtypeStruct((samples, head_count, rows, rows), BF16),
            jax.ShapeDtypeStruct((samples, head_count, head_width, rows), F32),
            jax.ShapeDtypeStruct((samples, head_count, 8, rows), F32),
        ],
        compiler_params=params("arbitrary", "arbitrary"),
    )(qt, k, vt)


def attend_kernel(
    first_pair, head_width, scale, mask_ref, e_ref, o_ref, st_ref, qt_ref, dot_ref, ko_ref, vo_ref, kto_ref, kp_ref, vp_ref, ktp_ref,
    vtp_ref, ctx_ref, dqt_ref, dko_ref, dvo_ref, dkp_ref, dvp_ref,
):
    pair = first_pair + pl.program_id(0)
    sections = mask_ref.shape[0]
    sub = kp_ref.shape[1] // sections
    ko, vo, kp, vp = ko_ref[0], vo_ref[0], kp_ref[0], vp_ref[0]
    dko = dvo = dkp = dvp = None
    for which in range(2):
        rows = slice(which * head_width, (which + 1) * head_width)
        q_half = head_rows(qt_ref[0], which, head_width)
        s = nn(kp, q_half)
        top_own = st_ref[0, which, 0:1, :]
        total_own = st_ref[0, which, 1:2, :]
        offs = [jnp.where(mask_ref[i, 2 * pair + which] > 0, 0.0, OFF).astype(F32) for i in range(sections)]
        top = top_own
        for i in range(sections):
            top = jnp.maximum(top, jnp.max(s[i * sub : (i + 1) * sub], axis=0, keepdims=True) - offs[i])
        e_part = jnp.concatenate([jnp.exp(s[i * sub : (i + 1) * sub] - (top + offs[i])) for i in range(sections)], 0)
        fade = jnp.exp(top_own - top)
        total = fade * total_own + jnp.sum(e_part, axis=0, keepdims=True)
        e_part = e_part.astype(BF16)
        e_own = e_ref[0, which]
        inverse = 1.0 / total
        o = fade * o_ref[0, which] + nn(vtp_ref[0, rows, :], e_part)
        ctx = (o * inverse).astype(BF16)
        ctx_ref[0, rows, :] = ctx
        ctx = ctx.astype(F32)
        g = dot_ref[0, rows, :].astype(F32)
        g_part = (g * inverse).astype(BF16)
        g_own = (g * (inverse * fade)).astype(BF16)
        r_part = jnp.sum(g_part.astype(F32) * ctx, axis=0, keepdims=True)
        r_own = jnp.sum(g_own.astype(F32) * ctx, axis=0, keepdims=True)
        blank = jnp.zeros_like(g_part)
        g_part = jnp.concatenate([g_part, blank] if which == 0 else [blank, g_part], 0)
        g_own = jnp.concatenate([g_own, blank] if which == 0 else [blank, g_own], 0)
        ds_part = ((nn(vp, g_part) - r_part).astype(BF16) * e_part)
        ds_own = ((nn(vo, g_own) - r_own).astype(BF16) * e_own)
        dqt_ref[0, rows, :] = ((nn(kto_ref[0, rows, :], ds_own) + nn(ktp_ref[0, rows, :], ds_part)) * scale).astype(BF16)
        terms = (nt(ds_own, q_half), nt(e_own, g_own), nt(ds_part, q_half), nt(e_part, g_part))
        if which == 0:
            dko, dvo, dkp, dvp = terms
        else:
            dko, dvo, dkp, dvp = dko + terms[0], dvo + terms[1], dkp + terms[2], dvp + terms[3]
    dko_ref[0] = dko.astype(BF16)
    dvo_ref[0] = dvo.astype(BF16)
    dkp_ref[0] = dkp.astype(BF16)
    dvp_ref[0] = dvp.astype(BF16)


def attend(group, groups, head_masks, own, qt, dot, ko, vo, kto, partner_rows, head_count, scale):
    e, o, st = own
    kp, vp, ktp, vtp = partner_rows
    samples, width, rows = qt.shape
    head_width = width // head_count
    pairs = head_count // 2 // groups
    first = group * pairs
    col_in = pl.BlockSpec((1, 2 * head_width, rows), lambda p, s: (s, first + p, 0))
    row_in = pl.BlockSpec((1, rows, 2 * head_width), lambda p, s: (s, 0, first + p))
    col_out = pl.BlockSpec((1, 2 * head_width, rows), lambda p, s: (s, p, 0))
    row_out = pl.BlockSpec((1, rows, 2 * head_width), lambda p, s: (s, 0, p))

    def per_head(n):
        return pl.BlockSpec((1, 2, n, rows), lambda p, s: (s, first + p, 0, 0))

    by_col = jax.ShapeDtypeStruct((samples, width // groups, rows), BF16)
    by_row = jax.ShapeDtypeStruct((samples, rows, width // groups), BF16)
    return pl.pallas_call(
        functools.partial(attend_kernel, first, head_width, scale),
        grid=(pairs, samples),
        in_specs=[pl.BlockSpec(memory_space=pltpu.SMEM), per_head(rows), per_head(head_width), per_head(8)]
        + [col_in, col_in, row_in, row_in, col_in, row_in, row_in, col_in, col_in],
        out_specs=[col_out, col_out] + [row_out] * 4,
        out_shape=[by_col, by_col] + [by_row] * 4,
        compiler_params=params("arbitrary", "arbitrary"),
    )(head_masks, e, o, st, qt, dot, ko, vo, kto, kp, vp, ktp, vtp)


def weights_kernel(place_ref, x_ref, x0, x1, x2, x3, c_ref, ctx_ref, dqt_ref, dko_ref, dvo_ref, dkp_ref, dvp_ref, keep_ref, send_ref, all_ref):
    samples, rows, width = x_ref.shape
    cols = dko_ref.shape[2]
    chunk = keep_ref.shape[1]
    chunks = 2 * keep_ref.shape[0]
    per_type = chunks // 4

    def put(kind, value):
        for i in range(per_type):
            all_ref[(kind * per_type + i) ^ place_ref[0]] = value[i * chunk : (i + 1) * chunk].astype(BF16)

    own = samples * rows
    x_all = jnp.concatenate([x_ref[s] for s in range(samples)] + [x[s] for s in range(samples) for x in (x0, x1, x2, x3)], 0)
    xt = x_all.T
    ctx = jnp.concatenate([ctx_ref[s] for s in range(samples)], 1)
    go = nn(ctx, c_ref[...].reshape(own, width))
    put(3, jnp.concatenate([go[:, i : i + cols] for i in range(0, width, cols)], 0))
    dqt = jnp.concatenate([dqt_ref[s] for s in range(samples)], 1)
    put(0, nt(xt[:, :own], dqt))
    dk = jnp.concatenate([dko_ref[s] for s in range(samples)] + [dkp_ref[s] for s in range(samples)], 0)
    put(1, nn(xt, dk))
    dv = jnp.concatenate([dvo_ref[s] for s in range(samples)] + [dvp_ref[s] for s in range(samples)], 0)
    put(2, nn(xt, dv))
    keep_ref[...] = all_ref[: chunks // 2]
    send_ref[...] = all_ref[chunks // 2 :]


def weight_grads(place, devices, tokens, arrived, cotangent, parts):
    width = tokens.shape[2]
    cols = parts[0].shape[1]
    half = jax.ShapeDtypeStruct((devices // 2, 4 * width // devices, cols), BF16)
    whole = pl.BlockSpec(memory_space=pltpu.VMEM)
    return pl.pallas_call(
        weights_kernel,
        in_specs=[pl.BlockSpec(memory_space=pltpu.SMEM)] + [whole] * 12,
        out_shape=[half, half],
        scratch_shapes=[pltpu.VMEM((devices, 4 * width // devices, cols), BF16)],
        compiler_params=params(),
    )(place, tokens, *arrived, cotangent, *parts)


def plan_of(levels):
    return [[0], [1]] + [list(range(low, min(low + 2, levels))) for low in range(2, levels, 2)]


def spread(number, bits):
    return sum((number >> at & 1) << bit for at, bit in enumerate(bits))


def place_of(plan):
    index = lax.axis_index("tok")
    place = jnp.int32(0)
    for bits in plan:
        digit = sum((index >> bit & 1) << at for at, bit in enumerate(bits))
        place = (place << len(bits)) + digit
    return place.reshape(1)


def exchange(x, mask):
    return lax.ppermute(x, "tok", [(i, i ^ mask) for i in range(lax.axis_size("tok"))])


def reduce_all(plan, keep, send):
    sends = [send]
    kept = keep
    for number, bits in enumerate(plan):
        came = [exchange(piece, spread(m + 1, bits)) for m, piece in enumerate(sends)]
        total = kept.astype(F32)
        for piece in came:
            total = total + piece.astype(F32)
        if number + 1 < len(plan):
            share = total.shape[0] >> len(plan[number + 1])
            parts = [total[i : i + share].astype(BF16) for i in range(0, total.shape[0], share)]
            kept, sends = parts[0], parts[1:]
        else:
            kept = total.astype(BF16)
    pieces = [kept]
    for bits in reversed(plan):
        mine = pieces[0] if len(pieces) == 1 else jnp.concatenate(pieces, 0)
        pieces = [mine] + [exchange(mine, spread(m, bits)) for m in range(1, 1 << len(bits))]
    return pieces


def spread_kernel(groups, count, place_ref, *refs):
    piece_refs, out_refs, all_ref = refs[: groups * count], refs[groups * count : -1], refs[-1]
    kinds, per_type, chunk, width = 4, all_ref.shape[0] // 4, all_ref.shape[1], all_ref.shape[2]
    cols = width // groups
    for g in range(groups):
        slot = 0
        for ref in piece_refs[g * count : (g + 1) * count]:
            for i in range(ref.shape[0]):
                all_ref[slot ^ place_ref[0], :, g * cols : (g + 1) * cols] = ref[i].astype(F32)
                slot += 1
    for kind in range(3):
        out_refs[kind][...] = all_ref[kind * per_type : (kind + 1) * per_type].reshape(width, width)
    last = all_ref[3 * per_type :].reshape(groups, cols, width)
    for g in range(groups):
        for i in range(groups):
            out_refs[3][g * cols : (g + 1) * cols, i * cols : (i + 1) * cols] = last[i, :, g * cols : (g + 1) * cols]


def spread_grads(place, devices, width, pieces):
    groups, count = len(pieces), len(pieces[0])
    whole = pl.BlockSpec(memory_space=pltpu.VMEM)
    return pl.pallas_call(
        functools.partial(spread_kernel, groups, count),
        in_specs=[pl.BlockSpec(memory_space=pltpu.SMEM)] + [whole] * (groups * count),
        out_shape=[jax.ShapeDtypeStruct((width, width), F32)] * 4,
        scratch_shapes=[pltpu.VMEM((devices, 4 * width // devices, width), F32)],
        compiler_params=params(),
    )(place, *[piece for group in pieces for piece in group])


def back_kernel(groups, *refs):
    dks, dvs = refs[:groups], refs[groups : 2 * groups]
    wk_ref, wv_ref, *outs = refs[2 * groups :]
    dk = jnp.concatenate([r[0] for r in dks], 1)
    dv = jnp.concatenate([r[0] for r in dvs], 1)
    total = (nt(dk, wk_ref[...]) + nt(dv, wv_ref[...])).astype(BF16)
    sub = outs[0].shape[1]
    for i, out in enumerate(outs):
        out[0] = total[i * sub : (i + 1) * sub]


def back(dkps, dvps, w_key, w_value):
    groups = len(dkps)
    samples, rows, cols = dkps[0].shape
    width = w_key.shape[0]
    part = pl.BlockSpec((1, rows, cols), lambda s: (s, 0, 0))
    whole = pl.BlockSpec((width, width), lambda s: (0, 0))
    return pl.pallas_call(
        functools.partial(back_kernel, groups),
        grid=(samples,),
        in_specs=[part] * (2 * groups) + [whole] * 2,
        out_specs=[pl.BlockSpec((1, rows // 4, width), lambda s: (s, 0, 0))] * 4,
        out_shape=[jax.ShapeDtypeStruct((samples, rows // 4, width), BF16)] * 4,
        compiler_params=params("arbitrary"),
    )(*dkps, *dvps, w_key, w_value)


def finish_kernel(groups, *refs):
    ctxs, dqts, dks, dvs = (refs[i * groups : (i + 1) * groups] for i in range(4))
    wo_ref, wq_ref, wk_ref, wv_ref, out_ref, gt_ref = refs[4 * groups :]
    ctx = jnp.concatenate([r[0] for r in ctxs], 0)
    out_ref[0] = tn(ctx, wo_ref[...]).astype(BF16)
    dqt = jnp.concatenate([r[0] for r in dqts], 0)
    dk = jnp.concatenate([r[0] for r in dks], 1)
    dv = jnp.concatenate([r[0] for r in dvs], 1)
    gt_ref[0] = tt(dqt, wq_ref[...]) + nt(dk, wk_ref[...]) + nt(dv, wv_ref[...])


def finish(ctxs, dqts, dks, dvs, w_out, w_query, w_key, w_value):
    groups = len(ctxs)
    samples, cols, rows = ctxs[0].shape
    width = w_out.shape[0]
    part = pl.BlockSpec((1, cols, rows), lambda s: (s, 0, 0))
    row_part = pl.BlockSpec((1, rows, cols), lambda s: (s, 0, 0))
    whole = pl.BlockSpec((width, width), lambda s: (0, 0))
    row_block = pl.BlockSpec((1, rows, width), lambda s: (s, 0, 0))
    return pl.pallas_call(
        functools.partial(finish_kernel, groups),
        grid=(samples,),
        in_specs=[part] * (2 * groups) + [row_part] * (2 * groups) + [whole] * 4,
        out_specs=[row_block, row_block],
        out_shape=[jax.ShapeDtypeStruct((samples, rows, width), BF16), jax.ShapeDtypeStruct((samples, rows, width), F32)],
        compiler_params=params("arbitrary"),
    )(*ctxs, *dqts, *dks, *dvs, w_out, w_query, w_key, w_value)


def token_kernel(start_ref, gt_ref, b0, b1, b2, b3, out_ref, acc_ref):
    sub = b0.shape[1]
    acc_ref[...] = gt_ref[0]
    for section, came in enumerate((b0, b1, b2, b3)):
        acc_ref[pl.ds(pl.multiple_of(start_ref[section] * sub, sub), sub), :] += came[0].astype(F32)
    out_ref[0] = acc_ref[...].astype(BF16)


def token_grads(starts, partial, backs):
    samples, rows, width = partial.shape
    row_block = pl.BlockSpec((1, rows, width), lambda s: (s, 0, 0))
    came = pl.BlockSpec((1,) + backs[0].shape[1:], lambda s: (s, 0, 0))
    return pl.pallas_call(
        token_kernel,
        grid=(samples,),
        in_specs=[pl.BlockSpec(memory_space=pltpu.SMEM), row_block] + [came] * 4,
        out_specs=row_block,
        out_shape=jax.ShapeDtypeStruct((samples, rows, width), BF16),
        scratch_shapes=[pltpu.VMEM((rows, width), F32)],
        compiler_params=params("arbitrary"),
    )(starts, partial, *backs)


def per_device(tokens, w_query, w_key, w_value, w_out, partner_block, head_masks, cotangent):
    samples, rows, width = tokens.shape
    head_count = head_masks.shape[2]
    devices = lax.axis_size("tok")
    levels = devices.bit_length() - 1
    plan = plan_of(levels)
    place = place_of(plan)
    scale = (width // head_count) ** -0.5
    theirs = [partner(partner_block, levels - 4 + section)[0, section] for section in range(4)]
    qt, ko, vo, kto, vto, dot = project(tokens, cotangent, w_query, w_key, w_value, w_out, scale)
    arrived = [
        partner(lax.dynamic_slice_in_dim(tokens, theirs[section] * SUB, SUB, 1), levels - 4 + section) for section in range(4)
    ]
    own = own_part(qt, ko, vto, head_count)
    partner_rows = project_partner(arrived, w_key, w_value)
    done, sums = [], []
    for group in range(GROUPS):
        parts = attend(group, GROUPS, head_masks[0], own, qt, dot, ko, vo, kto, partner_rows, head_count, scale)
        done.append(parts)
        sums.append(reduce_all(plan, *weight_grads(place, devices, tokens, arrived, cotangent, parts)))
    ctxs, dqts, dkos, dvos, dkps, dvps = zip(*done)
    backs = [partner(piece, levels - 4 + i) for i, piece in enumerate(back(dkps, dvps, w_key, w_value))]
    output, partial = finish(ctxs, dqts, dkos, dvos, w_out, w_query, w_key, w_value)
    grad_tokens = token_grads(jnp.stack(theirs), partial, backs)
    return (output, grad_tokens, *spread_grads(place, devices, width, sums))


def solution(mesh):
    rows = P("groups", "tok", None)
    placed = (rows, P(), P(), P(), P(), P("tok", None), P("tok", None, None), rows)
    grads = P("groups", None)
    return jax.shard_map(
        per_device, mesh=mesh, in_specs=placed, out_specs=(rows, rows, grads, grads, grads, grads), check_vma=False
    )
```

```python
import functools

import jax
import jax.numpy as jnp
from jax import lax
from jax.experimental import pallas as pl
from jax.experimental.pallas import tpu as pltpu
from jax.sharding import PartitionSpec as P

SUB = 128
CHUNKS = ((0, 1), (2, 3))
VMEM = 24 * 1024 * 1024
F32 = jnp.float32
BF16 = jnp.bfloat16
OFF = 1e30


def partner(x, stride):
    return lax.ppermute(x, "tok", [(i, i ^ 1 << stride) for i in range(lax.axis_size("tok"))])


def nn(a, b):
    return lax.dot_general(a, b, (((1,), (0,)), ((), ())), preferred_element_type=F32)


def nt(a, b):
    return lax.dot_general(a, b, (((1,), (1,)), ((), ())), preferred_element_type=F32)


def tn(a, b):
    return lax.dot_general(a, b, (((0,), (0,)), ((), ())), preferred_element_type=F32)


def tt(a, b):
    return lax.dot_general(a, b, (((0,), (1,)), ((), ())), preferred_element_type=F32)


def params(*semantics):
    return pltpu.CompilerParams(vmem_limit_bytes=VMEM, dimension_semantics=semantics or None)


def cost(us):
    return pl.CostEstimate(flops=int(us * 1.1e9), bytes_accessed=int(us * 1e5), transcendentals=0)


def far(*arrays):
    return [pltpu.with_memory_space_constraint(x, pltpu.HBM) for x in arrays]


def head_rows(pair_rows, which, head_width):
    row = lax.broadcasted_iota(jnp.int32, pair_rows.shape, 0)
    keep = (row >= which * head_width) & (row < (which + 1) * head_width)
    return jnp.where(keep, pair_rows, jnp.zeros_like(pair_rows))


def project_kernel(scale, x_ref, c_ref, wq_ref, wk_ref, wv_ref, wo_ref, qt_ref, k_ref, v_ref, kt_ref, vt_ref, dot_ref, xt_ref):
    x = x_ref[0]
    xt_ref[0] = x.T
    qt_ref[0] = (tt(wq_ref[...], x).astype(BF16).astype(F32) * scale).astype(BF16)
    k = nn(x, wk_ref[...])
    v = nn(x, wv_ref[...])
    k_ref[0] = k.astype(BF16)
    v_ref[0] = v.astype(BF16)
    kt_ref[0] = k.T.astype(BF16)
    vt_ref[0] = v.T.astype(BF16)
    dot_ref[0] = nt(wo_ref[...], c_ref[0]).astype(BF16)


def project(tokens, cotangent, w_query, w_key, w_value, w_out, scale):
    samples, rows, width = tokens.shape
    row_block = pl.BlockSpec((1, rows, width), lambda s: (s, 0, 0))
    col_block = pl.BlockSpec((1, width, rows), lambda s: (s, 0, 0))
    whole = pl.BlockSpec((width, width), lambda s: (0, 0))
    by_row = pltpu.VMEM((samples, rows, width), BF16)
    by_col = pltpu.VMEM((samples, width, rows), BF16)
    far_row = pltpu.HBM((samples, rows, width), BF16)
    far_col = pltpu.HBM((samples, width, rows), BF16)
    return pl.pallas_call(
        functools.partial(project_kernel, scale),
        grid=(samples,),
        in_specs=[row_block, row_block] + [whole] * 4,
        out_specs=[col_block, row_block, row_block, col_block, col_block, col_block, col_block],
        out_shape=[by_col, by_row, far_row, far_col, by_col, far_col, far_col],
        cost_estimate=cost(5),
        compiler_params=params("arbitrary"),
    )(*far(tokens, cotangent, w_query, w_key, w_value, w_out))


def project_partner_kernel(x0, x1, x2, x3, wk_ref, wv_ref, k_ref, v_ref, kt_ref, vt_ref, xt_ref):
    x = jnp.concatenate([x0[0], x1[0], x2[0], x3[0]], 0)
    xt_ref[0] = x.T
    k = nn(x, wk_ref[...])
    v = nn(x, wv_ref[...])
    k_ref[0] = k.astype(BF16)
    v_ref[0] = v.astype(BF16)
    kt_ref[0] = k.T.astype(BF16)
    vt_ref[0] = v.T.astype(BF16)


def project_partner(arrived, w_key, w_value):
    samples, sub_rows, width = arrived[0].shape
    rows = sub_rows * len(arrived)
    part = pl.BlockSpec((1, sub_rows, width), lambda s: (s, 0, 0))
    row_block = pl.BlockSpec((1, rows, width), lambda s: (s, 0, 0))
    col_block = pl.BlockSpec((1, width, rows), lambda s: (s, 0, 0))
    whole = pl.BlockSpec((width, width), lambda s: (0, 0))
    by_row = pltpu.VMEM((samples, rows, width), BF16)
    by_col = pltpu.VMEM((samples, width, rows), BF16)
    return pl.pallas_call(
        project_partner_kernel,
        grid=(samples,),
        in_specs=[part] * 4 + [whole] * 2,
        out_specs=[row_block, row_block, col_block, col_block, col_block],
        out_shape=[by_row, by_row, by_col, by_col, by_col],
        cost_estimate=cost(2.5),
        compiler_params=params("arbitrary"),
    )(*arrived, w_key, w_value)


def own_kernel(head_width, qt_ref, k_ref, vt_ref, e_ref, o_ref, st_ref):
    k = k_ref[0]
    for which in range(2):
        s = nn(k, head_rows(qt_ref[0], which, head_width))
        top = jnp.max(s, axis=0, keepdims=True)
        e = jnp.exp(s - top)
        total = jnp.sum(e, axis=0, keepdims=True)
        e = e.astype(BF16)
        e_ref[0, which] = e
        o_ref[0, which] = nn(vt_ref[0, which * head_width : (which + 1) * head_width, :], e)
        st_ref[0, which] = jnp.concatenate([top, total, jnp.zeros((6, top.shape[1]), F32)], 0)


def own_part(qt, k, vt, head_count):
    samples, width, rows = qt.shape
    head_width = width // head_count
    col_pair = pl.BlockSpec((1, 2 * head_width, rows), lambda p, s: (s, p, 0))
    row_pair = pl.BlockSpec((1, rows, 2 * head_width), lambda p, s: (s, 0, p))

    def per_head(n):
        return pl.BlockSpec((1, 2, n, rows), lambda p, s: (s, p, 0, 0))

    return pl.pallas_call(
        functools.partial(own_kernel, head_width),
        grid=(head_count // 2, samples),
        in_specs=[col_pair, row_pair, col_pair],
        out_specs=[per_head(rows), per_head(head_width), per_head(8)],
        out_shape=[
            pltpu.HBM((samples, head_count, rows, rows), BF16),
            pltpu.HBM((samples, head_count, head_width, rows), F32),
            pltpu.HBM((samples, head_count, 8, rows), F32),
        ],
        cost_estimate=cost(10),
        compiler_params=params("arbitrary", "arbitrary"),
    )(qt, k, vt)


def attend_kernel(
    pair, head_width, scale, mask_ref, e_ref, o_ref, st_ref, qt_ref, dot_ref, ko_ref, vo_ref, kto_ref, kp_ref, vp_ref, ktp_ref,
    vtp_ref, *refs,
):
    ctx_ref, dqt_ref, dko_ref, dvo_ref, dkp_ref, dvp_ref = refs[-6:]
    sections = mask_ref.shape[0]
    sub = kp_ref.shape[1] // sections
    ko, vo, kp, vp = ko_ref[0], vo_ref[0], kp_ref[0], vp_ref[0]
    dko = dvo = dkp = dvp = None
    for which in range(2):
        rows = slice(which * head_width, (which + 1) * head_width)
        q_half = head_rows(qt_ref[0], which, head_width)
        s = nn(kp, q_half)
        top_own = st_ref[0, which, 0:1, :]
        total_own = st_ref[0, which, 1:2, :]
        offs = [jnp.where(mask_ref[i, 2 * pair + which] > 0, 0.0, OFF).astype(F32) for i in range(sections)]
        top = top_own
        for i in range(sections):
            top = jnp.maximum(top, jnp.max(s[i * sub : (i + 1) * sub], axis=0, keepdims=True) - offs[i])
        e_part = jnp.concatenate([jnp.exp(s[i * sub : (i + 1) * sub] - (top + offs[i])) for i in range(sections)], 0)
        fade = jnp.exp(top_own - top)
        total = fade * total_own + jnp.sum(e_part, axis=0, keepdims=True)
        e_part = e_part.astype(BF16)
        e_own = e_ref[0, which]
        inverse = 1.0 / total
        o = fade * o_ref[0, which] + nn(vtp_ref[0, rows, :], e_part)
        ctx = (o * inverse).astype(BF16)
        ctx_ref[0, rows, :] = ctx
        ctx = ctx.astype(F32)
        g = dot_ref[0, rows, :].astype(F32)
        g_part = (g * inverse).astype(BF16)
        g_own = (g * (inverse * fade)).astype(BF16)
        r_part = jnp.sum(g_part.astype(F32) * ctx, axis=0, keepdims=True)
        r_own = jnp.sum(g_own.astype(F32) * ctx, axis=0, keepdims=True)
        blank = jnp.zeros_like(g_part)
        g_part = jnp.concatenate([g_part, blank] if which == 0 else [blank, g_part], 0)
        g_own = jnp.concatenate([g_own, blank] if which == 0 else [blank, g_own], 0)
        ds_part = ((nn(vp, g_part) - r_part).astype(BF16) * e_part)
        ds_own = ((nn(vo, g_own) - r_own).astype(BF16) * e_own)
        dqt_ref[0, rows, :] = ((nn(kto_ref[0, rows, :], ds_own) + nn(ktp_ref[0, rows, :], ds_part)) * scale).astype(BF16)
        terms = (nt(ds_own, q_half), nt(e_own, g_own), nt(ds_part, q_half), nt(e_part, g_part))
        if which == 0:
            dko, dvo, dkp, dvp = terms
        else:
            dko, dvo, dkp, dvp = dko + terms[0], dvo + terms[1], dkp + terms[2], dvp + terms[3]
    dko_ref[0] = dko.astype(BF16)
    dvo_ref[0] = dvo.astype(BF16)
    dkp_ref[0] = dkp.astype(BF16)
    dvp_ref[0] = dvp.astype(BF16)


def attend(pair, head_masks, own, qt, dot, ko, vo, kto, partner_rows, head_count, scale, after):
    e, o, st = own
    kp, vp, ktp, vtp = partner_rows
    samples, width, rows = qt.shape
    head_width = width // head_count
    col_in = pl.BlockSpec((1, 2 * head_width, rows), lambda s: (s, pair, 0))
    row_in = pl.BlockSpec((1, rows, 2 * head_width), lambda s: (s, 0, pair))
    col_out = pl.BlockSpec((1, 2 * head_width, rows), lambda s: (s, 0, 0))
    row_out = pl.BlockSpec((1, rows, 2 * head_width), lambda s: (s, 0, 0))

    def per_head(n):
        return pl.BlockSpec((1, 2, n, rows), lambda s: (s, pair, 0, 0))

    by_col = pltpu.VMEM((samples, 2 * head_width, rows), BF16)
    by_row = pltpu.VMEM((samples, rows, 2 * head_width), BF16)
    return pl.pallas_call(
        functools.partial(attend_kernel, pair, head_width, scale),
        grid=(samples,),
        in_specs=[pl.BlockSpec(memory_space=pltpu.SMEM), per_head(rows), per_head(head_width), per_head(8)]
        + [col_in, col_in, row_in, row_in, col_in, row_in, row_in, col_in, col_in]
        + [pl.BlockSpec(memory_space=pl.ANY)] * len(after),
        out_specs=[col_out, col_out] + [row_out] * 4,
        out_shape=[by_col, by_col] + [by_row] * 4,
        cost_estimate=cost(7),
        compiler_params=params("arbitrary"),
    )(head_masks, *far(e, o, st), qt, *far(dot), ko, *far(vo, kto), kp, vp, ktp, vtp, *after)


def weights_kernel(pairs, place_ref, xt_ref, xtp_ref, c_ref, *refs):
    ctxs, dqts, dkos, dvos, dkps, dvps = (refs[i * pairs : (i + 1) * pairs] for i in range(6))
    keep_ref, send_ref, all_ref = refs[-3:]
    samples, width, rows = xt_ref.shape
    cols = pairs * dkos[0].shape[2]
    chunk = keep_ref.shape[1]
    chunks = 2 * keep_ref.shape[0]
    per_type = chunks // 4

    def put(kind, value):
        for i in range(per_type):
            all_ref[(kind * per_type + i) ^ place_ref[0]] = value[i * chunk : (i + 1) * chunk].astype(BF16)

    xt = jnp.concatenate([xt_ref[s] for s in range(samples)], 1)
    xt_all = jnp.concatenate([xt_ref[s] for s in range(samples)] + [xtp_ref[s] for s in range(samples)], 1)

    def across(parts):
        return jnp.concatenate([jnp.concatenate([r[s] for r in parts], 0) for s in range(samples)], 1)

    def down(parts):
        return [jnp.concatenate([r[s] for r in parts], 1) for s in range(samples)]

    go = nn(across(ctxs), c_ref[...].reshape(samples * rows, width))
    put(3, jnp.concatenate([go[:, i : i + cols] for i in range(0, width, cols)], 0))
    put(0, nt(xt, across(dqts)))
    put(1, nn(xt_all, jnp.concatenate(down(dkos) + down(dkps), 0)))
    put(2, nn(xt_all, jnp.concatenate(down(dvos) + down(dvps), 0)))
    keep_ref[...] = all_ref[: chunks // 2]
    send_ref[...] = all_ref[chunks // 2 :]


def weight_grads(place, devices, xt, xtp, cotangent, parts, after):
    samples, width, rows = xt.shape
    pairs = len(parts[0])
    cols = pairs * parts[0][0].shape[1]
    half = pltpu.VMEM((devices // 2, 4 * width // devices, cols), BF16)
    whole = pl.BlockSpec(memory_space=pltpu.VMEM)
    return pl.pallas_call(
        functools.partial(weights_kernel, pairs),
        in_specs=[pl.BlockSpec(memory_space=pltpu.SMEM)] + [pl.BlockSpec(xt.shape, lambda: (0, 0, 0)), whole, pl.BlockSpec(cotangent.shape, lambda: (0, 0, 0))] + [whole] * (6 * pairs) + [pl.BlockSpec(memory_space=pl.ANY)] * len(after),
        out_shape=[half, half],
        scratch_shapes=[pltpu.VMEM((devices, 4 * width // devices, cols), BF16)],
        cost_estimate=cost(3),
        compiler_params=params(),
    )(place, *far(xt), xtp, *far(cotangent), *[x for part in parts for x in part], *after)


def plan_of(levels):
    return [[0], [1]] + [list(range(low, min(low + 2, levels))) for low in range(2, levels, 2)]


def spread(number, bits):
    return sum((number >> at & 1) << bit for at, bit in enumerate(bits))


def place_of(plan):
    index = lax.axis_index("tok")
    place = jnp.int32(0)
    for bits in plan:
        digit = sum((index >> bit & 1) << at for at, bit in enumerate(bits))
        place = (place << len(bits)) + digit
    return place.reshape(1)


def exchange(x, mask):
    return lax.ppermute(x, "tok", [(i, i ^ mask) for i in range(lax.axis_size("tok"))])


def fold(kept, came, share):
    total = kept.astype(F32)
    for piece in came:
        total = total + piece.astype(F32)
    parts = [total[i : i + share].astype(BF16) for i in range(0, total.shape[0], share)]
    return parts[0], parts[1:]


def send_all(pieces, bits):
    return [exchange(piece, spread(m + 1, bits)) for m, piece in enumerate(pieces)]


def gather_all(mine, bits):
    return [mine] + [exchange(mine, spread(m, bits)) for m in range(1, 1 << len(bits))]


def tie(*values):
    return lax.optimization_barrier(values)


def spread_kernel(groups, place_ref, *refs):
    piece_refs, out_refs, all_ref = refs[:-5], refs[-5:-1], refs[-1]
    per_type, width = all_ref.shape[0] // 4, all_ref.shape[2]
    cols = width // groups
    slot = 0
    for ref in piece_refs:
        for i in range(ref.shape[0]):
            all_ref[slot ^ place_ref[0]] = ref[i].astype(F32)
            slot += 1
    for kind in range(3):
        out_refs[kind][...] = all_ref[kind * per_type : (kind + 1) * per_type].reshape(width, width)
    last = all_ref[3 * per_type :].reshape(groups, cols, width)
    for g in range(groups):
        for i in range(groups):
            out_refs[3][g * cols : (g + 1) * cols, i * cols : (i + 1) * cols] = last[i, :, g * cols : (g + 1) * cols]


def spread_grads(place, devices, width, pieces):
    whole = pl.BlockSpec(memory_space=pltpu.VMEM)
    return pl.pallas_call(
        functools.partial(spread_kernel, len(CHUNKS)),
        in_specs=[pl.BlockSpec(memory_space=pltpu.SMEM)] + [whole] * len(pieces),
        out_shape=[jax.ShapeDtypeStruct((width, width), F32)] * 4,
        scratch_shapes=[pltpu.VMEM((devices, 4 * width // devices, width), F32)],
        compiler_params=params(),
    )(place, *pieces)


def back_kernel(groups, *refs):
    dks, dvs = refs[:groups], refs[groups : 2 * groups]
    wk_ref, wv_ref, *outs = refs[2 * groups :]
    dk = jnp.concatenate([r[0] for r in dks], 1)
    dv = jnp.concatenate([r[0] for r in dvs], 1)
    total = (nt(dk, wk_ref[...]) + nt(dv, wv_ref[...])).astype(BF16)
    sub = outs[0].shape[1]
    for i, out in enumerate(outs):
        out[0] = total[i * sub : (i + 1) * sub]


def back(dkps, dvps, w_key, w_value):
    groups = len(dkps)
    samples, rows, cols = dkps[0].shape
    width = w_key.shape[0]
    part = pl.BlockSpec((1, rows, cols), lambda s: (s, 0, 0))
    whole = pl.BlockSpec((width, width), lambda s: (0, 0))
    return pl.pallas_call(
        functools.partial(back_kernel, groups),
        grid=(samples,),
        in_specs=[part] * (2 * groups) + [whole] * 2,
        out_specs=[pl.BlockSpec((1, rows // 4, width), lambda s: (s, 0, 0))] * 4,
        out_shape=[pltpu.VMEM((samples, rows // 4, width), BF16)] * 4,
        cost_estimate=cost(1.7),
        compiler_params=params("arbitrary"),
    )(*dkps, *dvps, w_key, w_value)


def finish_kernel(groups, *refs):
    ctxs, dqts, dks, dvs = (refs[i * groups : (i + 1) * groups] for i in range(4))
    wo_ref, wq_ref, wk_ref, wv_ref, out_ref, gt_ref = refs[4 * groups :]
    ctx = jnp.concatenate([r[0] for r in ctxs], 0)
    out_ref[0] = tn(ctx, wo_ref[...]).astype(BF16)
    dqt = jnp.concatenate([r[0] for r in dqts], 0)
    dk = jnp.concatenate([r[0] for r in dks], 1)
    dv = jnp.concatenate([r[0] for r in dvs], 1)
    gt_ref[0] = tt(dqt, wq_ref[...]) + nt(dk, wk_ref[...]) + nt(dv, wv_ref[...])


def finish(ctxs, dqts, dks, dvs, w_out, w_query, w_key, w_value):
    groups = len(ctxs)
    samples, cols, rows = ctxs[0].shape
    width = w_out.shape[0]
    part = pl.BlockSpec((1, cols, rows), lambda s: (s, 0, 0))
    row_part = pl.BlockSpec((1, rows, cols), lambda s: (s, 0, 0))
    whole = pl.BlockSpec((width, width), lambda s: (0, 0))
    row_block = pl.BlockSpec((1, rows, width), lambda s: (s, 0, 0))
    return pl.pallas_call(
        functools.partial(finish_kernel, groups),
        grid=(samples,),
        in_specs=[part] * (2 * groups) + [row_part] * (2 * groups) + [whole] * 4,
        out_specs=[row_block, row_block],
        out_shape=[jax.ShapeDtypeStruct((samples, rows, width), BF16), pltpu.VMEM((samples, rows, width), F32)],
        cost_estimate=cost(4),
        compiler_params=params("arbitrary"),
    )(*ctxs, *dqts, *dks, *dvs, w_out, w_query, w_key, w_value)


def token_kernel(i0, i1, i2, i3, gt_ref, b0, b1, b2, b3, out_ref, acc_ref):
    sub = b0.shape[1]
    acc_ref[...] = gt_ref[0]
    for section, (index, came) in enumerate(((i0, b0), (i1, b1), (i2, b2), (i3, b3))):
        acc_ref[pl.ds(pl.multiple_of(index[0, section] * sub, sub), sub), :] += came[0].astype(F32)
    out_ref[0] = acc_ref[...].astype(BF16)


def token_grads(starts, partial, backs):
    samples, rows, width = partial.shape
    row_block = pl.BlockSpec((1, rows, width), lambda s: (s, 0, 0))
    came = pl.BlockSpec((1,) + backs[0].shape[1:], lambda s: (s, 0, 0))
    return pl.pallas_call(
        token_kernel,
        grid=(samples,),
        in_specs=[pl.BlockSpec(memory_space=pltpu.SMEM)] * 4 + [row_block] + [came] * 4,
        out_specs=row_block,
        out_shape=jax.ShapeDtypeStruct((samples, rows, width), BF16),
        scratch_shapes=[pltpu.VMEM((rows, width), F32)],
        compiler_params=params("arbitrary"),
    )(*starts, partial, *backs)


def pick_kernel(i0, i1, i2, i3, x_ref, o0, o1, o2, o3):
    sub = o0.shape[1]
    for section, (index, out) in enumerate(((i0, o0), (i1, o1), (i2, o2), (i3, o3))):
        out[...] = x_ref[:, pl.ds(pl.multiple_of(index[0, section] * sub, sub), sub), :]


def pick(starts, tokens):
    samples, _, width = tokens.shape
    return pl.pallas_call(
        pick_kernel,
        in_specs=[pl.BlockSpec(memory_space=pltpu.SMEM)] * 4 + [pl.BlockSpec(tokens.shape, lambda: (0, 0, 0))],
        out_shape=[pltpu.VMEM((samples, SUB, width), BF16)] * 4,
        cost_estimate=cost(1),
        compiler_params=params(),
    )(*starts, *far(tokens))


def per_device(tokens, w_query, w_key, w_value, w_out, partner_block, head_masks, cotangent):
    samples, rows, width = tokens.shape
    head_count = head_masks.shape[2]
    devices = lax.axis_size("tok")
    levels = devices.bit_length() - 1
    plan = plan_of(levels)
    place = place_of(plan)
    scale = (width // head_count) ** -0.5
    theirs = [partner(partner_block, levels - 4 + section) for section in range(4)]
    qt, ko, vo, kto, vto, dot, xt = project(tokens, cotangent, w_query, w_key, w_value, w_out, scale)
    arrived = [partner(piece, levels - 4 + section) for section, piece in enumerate(pick(theirs, tokens))]
    own = own_part(qt, ko, vto, head_count)
    *partner_rows, xtp = project_partner(arrived, w_key, w_value)
    def run(pair, after=()):
        return attend(pair, head_masks[0], own, qt, dot, ko, vo, kto, partner_rows, head_count, scale, after)

    def weigh(parts, after=()):
        return weight_grads(place, devices, xt, xtp, cotangent, list(zip(*parts)), after)

    first = [run(pair) for pair in CHUNKS[0]]
    kept0, sends0 = weigh(first)
    came = send_all([sends0], plan[0])
    second = [run(CHUNKS[1][0], (sends0,))]
    kept0, sends0 = fold(kept0, came, devices // 4)
    came = send_all(sends0, plan[1])
    second.append(run(CHUNKS[1][1], sends0))
    kept0, _ = fold(kept0, came, devices // 4)
    kept, sends = weigh(second, (kept0,))
    ctxs, dqts, dkos, dvos, dkps, dvps = zip(*(first + second))
    came = send_all([sends], plan[0])
    backs = back(dkps, dvps, w_key, w_value)
    kept, sends = fold(kept, came, devices // 4)
    came, *backs = tie(*send_all(sends, plan[1]), *backs)
    backs = [partner(piece, levels - 4 + i) for i, piece in enumerate(backs)]
    output, partial = finish(ctxs, dqts, dkos, dvos, w_out, w_query, w_key, w_value)
    kept, _ = fold(kept, [came], devices // 4)
    kept = jnp.concatenate([kept0, kept], 2)
    left = devices // 4
    for number in range(2, len(plan)):
        left >>= len(plan[number])
        sends = [kept[i : i + left] for i in range(0, kept.shape[0], left)]
        came = send_all(sends[1:], plan[number])
        if number == 2:
            *came, partial = tie(*came, partial)
        kept, _ = fold(sends[0], came, left)
    grad_tokens = token_grads(theirs, partial, backs)
    pieces = [kept]
    for number in reversed(range(len(plan))):
        mine = pieces[0] if len(pieces) == 1 else jnp.concatenate(pieces, 0)
        if number == 0:
            mine, grad_tokens = tie(mine, grad_tokens)
        pieces = gather_all(mine, plan[number])
    return (output, grad_tokens, *spread_grads(place, devices, width, pieces))


def solution(mesh):
    rows = P("groups", "tok", None)
    placed = (rows, P(), P(), P(), P(), P("tok", None), P("tok", None, None), rows)
    grads = P("groups", None)
    return jax.shard_map(
        per_device, mesh=mesh, in_specs=placed, out_specs=(rows, rows, grads, grads, grads, grads), check_vma=False
    )
```

```python
import functools

import jax
import jax.numpy as jnp
from jax import lax
from jax.experimental import pallas as pl
from jax.experimental.pallas import tpu as pltpu
from jax.sharding import PartitionSpec as P

SUB = 128
CHUNKS = ((0, 1), (2, 3))
VMEM = 14 * 1024 * 1024
F32 = jnp.float32
BF16 = jnp.bfloat16
OFF = 1e30
TILE = 128
DONE = object()


def partner(x, stride):
    return lax.ppermute(x, "tok", [(i, i ^ 1 << stride) for i in range(lax.axis_size("tok"))])


def nn(a, b):
    return lax.dot_general(a, b, (((1,), (0,)), ((), ())), preferred_element_type=F32)


def nt(a, b):
    return lax.dot_general(a, b, (((1,), (1,)), ((), ())), preferred_element_type=F32)


def tn(a, b):
    return lax.dot_general(a, b, (((0,), (0,)), ((), ())), preferred_element_type=F32)


def tt(a, b):
    return lax.dot_general(a, b, (((0,), (1,)), ((), ())), preferred_element_type=F32)


def params(*semantics):
    return pltpu.CompilerParams(vmem_limit_bytes=VMEM, dimension_semantics=semantics or None)


def cost(us):
    return pl.CostEstimate(flops=int(us * 1.1e9), bytes_accessed=int(us * 1e5), transcendentals=0)


def far(*arrays):
    return [pltpu.with_memory_space_constraint(x, pltpu.HBM) for x in arrays]


def near(*arrays):
    return [pltpu.with_memory_space_constraint(x, pltpu.VMEM) for x in arrays]


def head_rows(pair_rows, which, head_width):
    row = lax.broadcasted_iota(jnp.int32, pair_rows.shape, 0)
    keep = (row >= which * head_width) & (row < (which + 1) * head_width)
    return jnp.where(keep, pair_rows, jnp.zeros_like(pair_rows))


def project_kernel(scale, x_ref, c_ref, wq_ref, wk_ref, wv_ref, wo_ref, qt_ref, k_ref, v_ref, kt_ref, vt_ref, dot_ref, xt_ref):
    x = x_ref[0]
    xt_ref[0] = x.T
    qt_ref[0] = (tt(wq_ref[...], x).astype(BF16).astype(F32) * scale).astype(BF16)
    k = nn(x, wk_ref[...])
    v = nn(x, wv_ref[...])
    k_ref[0] = k.astype(BF16)
    v_ref[0] = v.astype(BF16)
    kt_ref[0] = k.T.astype(BF16)
    vt_ref[0] = v.T.astype(BF16)
    dot_ref[0] = nt(wo_ref[...], c_ref[0]).astype(BF16)


def project(tokens, cotangent, w_query, w_key, w_value, w_out, scale):
    samples, rows, width = tokens.shape
    row_block = pl.BlockSpec((1, rows, width), lambda s: (s, 0, 0))
    col_block = pl.BlockSpec((1, width, rows), lambda s: (s, 0, 0))
    whole = pl.BlockSpec((width, width), lambda s: (0, 0))
    by_row = pltpu.VMEM((samples, rows, width), BF16)
    by_col = pltpu.VMEM((samples, width, rows), BF16)
    far_row = pltpu.HBM((samples, rows, width), BF16)
    far_col = pltpu.HBM((samples, width, rows), BF16)
    return pl.pallas_call(
        functools.partial(project_kernel, scale),
        grid=(samples,),
        in_specs=[row_block, row_block] + [whole] * 4,
        out_specs=[col_block, row_block, row_block, col_block, col_block, col_block, col_block],
        out_shape=[by_col, by_row, far_row, far_col, by_col, far_col, far_col],
        cost_estimate=cost(5),
        compiler_params=params("arbitrary"),
    )(*far(tokens, cotangent, w_query, w_key, w_value, w_out))


def bring(sources, targets, sem):
    copies = [pltpu.make_async_copy(src, dst, sem.at[i]) for i, (src, dst) in enumerate(zip(sources, targets))]
    for copy in copies:
        copy.start()
    return copies


def project_partner_kernel(loads, x0, x1, x2, x3, wk_ref, wv_ref, *refs):
    k_ref, v_ref, kt_ref, vt_ref, xt_ref, *targets, sem = refs[-6 - loads :]
    sources = refs[:loads]
    copies = bring([sources[0].at[0], *sources[1:]], targets, sem)
    for s in range(x0.shape[0]):
        x = jnp.concatenate([x0[s], x1[s], x2[s], x3[s]], 0)
        xt_ref[s] = x.T
        k = nn(x, wk_ref[...])
        v = nn(x, wv_ref[...])
        k_ref[s] = k.astype(BF16)
        v_ref[s] = v.astype(BF16)
        kt_ref[s] = k.T.astype(BF16)
        vt_ref[s] = v.T.astype(BF16)
    for copy in copies:
        copy.wait()


def project_partner(arrived, w_key, w_value, loads, held):
    samples, sub_rows, width = arrived[0].shape
    rows = sub_rows * len(arrived)
    whole = pl.BlockSpec(memory_space=pltpu.VMEM)
    weight = pl.BlockSpec((width, width), lambda: (0, 0))
    anywhere = pl.BlockSpec(memory_space=pl.ANY)
    by_row = pltpu.VMEM((samples, rows, width), BF16)
    by_col = pltpu.VMEM((samples, width, rows), BF16)
    return pl.pallas_call(
        functools.partial(project_partner_kernel, len(loads)),
        in_specs=[whole] * 4 + [weight] * 2 + [anywhere] * len(loads) + [whole] * len(held),
        out_specs=[whole] * (5 + len(loads)),
        out_shape=[by_row, by_row, by_col, by_col, by_col, pltpu.VMEM(loads[0].shape[1:], BF16)]
        + [pltpu.VMEM(x.shape, x.dtype) for x in loads[1:]],
        scratch_shapes=[pltpu.SemaphoreType.DMA((len(loads),))],
        cost_estimate=cost(2.5),
        compiler_params=params(),
    )(*near(*arrived), *far(w_key, w_value, *loads), *near(*held))


def weave(*streams):
    streams = [iter(x) for x in streams]
    while streams:
        streams = [x for x in streams if next(x, DONE) is not DONE]


def down8(x, op):
    return op(x.reshape(x.shape[0] // 8, 8, x.shape[1]), axis=0)


def own_kernel(head_width, qt_ref, k_ref, vt_ref, *refs):
    loads = (len(refs) - 5) // 2
    e_ref, o_ref, st_ref, *targets, s_ref, sem = refs[loads:]
    copies = [pltpu.make_async_copy(src, dst, sem.at[i]) for i, (src, dst) in enumerate(zip(refs[:loads], targets))]

    @pl.when(pl.program_id(0) == 0)
    def _():
        for copy in copies:
            copy.start()

    samples, width, rows = qt_ref.shape
    units = [(sample, which) for sample in range(samples) for which in range(2)]

    def one_pair(pair):
        first = pl.multiple_of(pair * 2 * head_width, 2 * head_width)
        tops = {}

        def score(unit):
            sample, which = unit
            half = head_rows(qt_ref[sample, pl.ds(first, 2 * head_width), :], which, head_width)
            top = None
            for at in range(0, rows, TILE):
                s = nn(k_ref[sample, at : at + TILE, pl.ds(first, 2 * head_width)], half)
                s_ref[which, at : at + TILE, :] = s
                part = down8(s, jnp.max)
                top = part if top is None else jnp.maximum(top, part)
                yield
            tops[unit] = jnp.max(top, axis=0, keepdims=True)

        def expo(unit):
            sample, which = unit
            cols = slice(which * rows, (which + 1) * rows)
            total = None
            for at in range(0, rows, TILE):
                e = jnp.exp(s_ref[which, at : at + TILE, :] - tops[unit])
                part = down8(e, jnp.sum)
                total = part if total is None else total + part
                e_ref[0, sample, at : at + TILE, cols] = e.astype(BF16)
                yield
            total = jnp.sum(total, axis=0, keepdims=True)
            st_ref[sample, 2 * pair + which] = jnp.concatenate([tops[unit], total, jnp.zeros((6, rows), F32)], 0)

        def out(unit):
            sample, which = unit
            cols = slice(which * rows, (which + 1) * rows)
            span = pl.ds(first + which * head_width, head_width)
            o_ref[sample, 2 * pair + which] = nn(vt_ref[sample, span, :], e_ref[0, sample, :, cols])
            yield

        count = len(units)
        for i in range(count + 2):
            streams = []
            if i < count:
                streams.append(score(units[i]))
            if 1 <= i <= count:
                streams.append(expo(units[i - 1]))
            if i >= 2:
                streams.append(out(units[i - 2]))
            weave(*streams)

    one_pair(pl.program_id(0))

    @pl.when(pl.program_id(0) == pl.num_programs(0) - 1)
    def _():
        for copy in copies:
            copy.wait()


def own_part(qt, k, vt, head_count, loads):
    samples, width, rows = qt.shape
    head_width = width // head_count
    whole = pl.BlockSpec(memory_space=pltpu.VMEM)
    return pl.pallas_call(
        functools.partial(own_kernel, head_width),
        grid=(head_count // 2,),
        in_specs=[whole] * 3 + [pl.BlockSpec(memory_space=pl.ANY)] * len(loads),
        out_specs=[pl.BlockSpec((1, samples, rows, 2 * rows), lambda p: (p, 0, 0, 0))] + [whole] * (2 + len(loads)),
        out_shape=[
            pltpu.HBM((head_count // 2, samples, rows, 2 * rows), BF16),
            pltpu.VMEM((samples, head_count, head_width, rows), F32),
            pltpu.VMEM((samples, head_count, 8, rows), F32),
        ]
        + [pltpu.VMEM(x.shape, x.dtype) for x in loads],
        scratch_shapes=[pltpu.VMEM((2, rows, rows), F32), pltpu.SemaphoreType.DMA((len(loads),))],
        cost_estimate=cost(10),
        compiler_params=params("arbitrary"),
    )(*near(qt, k, vt), *far(*loads))


def attend_kernel(
    pair, head_width, scale, mask_ref, e_ref, o_ref, st_ref, qt_ref, dot_ref, vo_ref, kto_ref, kp_ref, vp_ref, ktp_ref,
    vtp_ref, *refs,
):
    s_ref, ep_ref, dsp_ref, dso_ref, ops_ref, sem = refs[-6:]
    loads = sem.shape[0]
    targets = refs[-6 - loads : -6]
    ctx_ref, dqt_ref, dko_ref, dvo_ref, dkp_ref, dvp_ref = refs[-12 - loads : -6 - loads]
    sources = [x.at[pair + 1] if len(x.shape) == 4 else x for x in refs[:loads]]
    copies = bring(sources, targets, sem)
    sections = mask_ref.shape[0]
    samples, _, rows = qt_ref.shape
    sub = kp_ref.shape[1] // sections
    both = slice(pair * 2 * head_width, (pair + 1) * 2 * head_width)
    stats = {}

    def span(which):
        return slice((2 * pair + which) * head_width, (2 * pair + which + 1) * head_width)

    def cols(which):
        return slice(which * rows, (which + 1) * rows)

    def score(unit):
        sample, which = unit
        kept = stats[unit] = {}
        kept["q"] = head_rows(qt_ref[sample, both, :], which, head_width)
        kept["g"] = head_rows(dot_ref[sample, both, :], which, head_width)
        kept["off"] = [jnp.where(mask_ref[i, 2 * pair + which] > 0, 0.0, OFF).astype(F32) for i in range(sections)]
        top = None
        for i in range(sections):
            at = slice(i * sub, (i + 1) * sub)
            s = nn(kp_ref[sample, at, both], kept["q"])
            s_ref[which, at, :] = s
            part = down8(s, jnp.max) - kept["off"][i]
            top = part if top is None else jnp.maximum(top, part)
            yield
        top_own = st_ref[sample, 2 * pair + which, 0:1, :]
        kept["top"] = jnp.maximum(top_own, jnp.max(top, axis=0, keepdims=True))
        kept["fade"] = jnp.exp(top_own - kept["top"])

    def expo(unit):
        sample, which = unit
        kept = stats[unit]
        total = None
        for i in range(sections):
            at = slice(i * sub, (i + 1) * sub)
            e = jnp.exp(s_ref[which, at, :] - (kept["top"] + kept["off"][i]))
            part = down8(e, jnp.sum)
            total = part if total is None else total + part
            ep_ref[sample, at, cols(which)] = e.astype(BF16)
            yield
        total = jnp.sum(total, axis=0, keepdims=True) + kept["fade"] * st_ref[sample, 2 * pair + which, 1:2, :]
        kept["inverse"] = 1.0 / total

    def blend(unit):
        sample, which = unit
        kept = stats[unit]
        inverse, fade = kept["inverse"], kept["fade"]
        here = slice(which * head_width, (which + 1) * head_width)
        o = fade * o_ref[sample, 2 * pair + which] + nn(vtp_ref[sample, span(which), :], ep_ref[sample, :, cols(which)])
        ctx = (o * inverse).astype(BF16)
        ctx_ref[sample, here, :] = ctx
        g = dot_ref[sample, span(which), :].astype(F32)
        kept["r"] = jnp.sum(g * ctx.astype(F32), axis=0, keepdims=True)
        q32, g32 = kept["q"].astype(F32), kept["g"].astype(F32)
        ops_ref[sample, 0, :, cols(which)] = (q32 * inverse).astype(BF16)
        ops_ref[sample, 1, :, cols(which)] = (g32 * inverse).astype(BF16)
        ops_ref[sample, 2, :, cols(which)] = (q32 * (inverse * fade)).astype(BF16)
        ops_ref[sample, 3, :, cols(which)] = (g32 * (inverse * fade)).astype(BF16)
        yield

    def slope(unit):
        sample, which = unit
        kept = stats[unit]
        for v_ref, get, put_ref in ((vp_ref, ep_ref.at[sample], dsp_ref), (vo_ref, e_ref.at[sample], dso_ref)):
            for lo in range(0, rows, TILE):
                at = slice(lo, lo + TILE)
                dp = nn(v_ref[sample, at, both], kept["g"]) - kept["r"]
                put_ref[sample, at, cols(which)] = dp.astype(BF16) * get[at, cols(which)]
                yield

    def query(unit):
        sample, which = unit
        kept = stats[unit]
        dq = nn(ktp_ref[sample, span(which), :], dsp_ref[sample, :, cols(which)])
        yield
        dq = dq + kept["fade"] * nn(kto_ref[sample, span(which), :], dso_ref[sample, :, cols(which)])
        here = slice(which * head_width, (which + 1) * head_width)
        dqt_ref[sample, here, :] = (dq * (kept["inverse"] * scale)).astype(BF16)

    def keys(sample):
        jobs = (
            (dvp_ref, ep_ref.at[sample], 1),
            (dvo_ref, e_ref.at[sample], 3),
            (dkp_ref, dsp_ref.at[sample], 0),
            (dko_ref, dso_ref.at[sample], 2),
        )
        for out_ref, left, number in jobs:
            for lo in range(0, rows, TILE):
                at = slice(lo, lo + TILE)
                out_ref[sample, at, :] = nt(left[at, :], ops_ref[sample, number]).astype(BF16)
                yield

    def chain(*streams):
        for stream in streams:
            yield from stream

    for sample in range(samples):
        one, two = (sample, 0), (sample, 1)
        before = keys(sample - 1) if sample else iter(())
        weave(score(one), before)
        weave(score(two), expo(one), before)
        weave(blend(one))
        weave(slope(one), expo(two), before)
        weave(blend(two), before)
        weave(slope(two), query(one), before)
        weave(query(two), before)
    weave(keys(samples - 1))
    for copy in copies:
        copy.wait()


def attend(pair, head_masks, e, stats, qt, dot, vo, kto, partner_rows, head_count, scale, loads, held, after):
    kp, vp, ktp, vtp = partner_rows
    samples, width, rows = qt.shape
    head_width = width // head_count
    whole = pl.BlockSpec(memory_space=pltpu.VMEM)
    anywhere = pl.BlockSpec(memory_space=pl.ANY)
    by_col = pltpu.VMEM((samples, 2 * head_width, rows), BF16)
    by_row = pltpu.VMEM((samples, rows, 2 * head_width), BF16)
    return pl.pallas_call(
        functools.partial(attend_kernel, pair, head_width, scale),
        in_specs=[pl.BlockSpec(memory_space=pltpu.SMEM)] + [whole] * 11 + [anywhere] * len(loads) + [whole] * len(held) + [anywhere] * len(after),
        out_specs=[whole] * (6 + len(loads)),
        out_shape=[by_col, by_col] + [by_row] * 4 + [pltpu.VMEM(x.shape[-4 + (x.ndim == 4) :], x.dtype) for x in loads],
        scratch_shapes=[
            pltpu.VMEM((2, rows, rows), F32),
            pltpu.VMEM((samples, rows, 2 * rows), BF16),
            pltpu.VMEM((samples, rows, 2 * rows), BF16),
            pltpu.VMEM((samples, rows, 2 * rows), BF16),
            pltpu.VMEM((samples, 4, 2 * head_width, 2 * rows), BF16),
            pltpu.SemaphoreType.DMA((max(len(loads), 1),)) if loads else pltpu.SemaphoreType.DMA((0,)),
        ],
        cost_estimate=cost(6),
        compiler_params=params(),
    )(head_masks, *near(e, *stats, qt, dot, vo, kto, kp, vp, ktp, vtp), *far(*loads), *near(*held), *after)


def weights_kernel(pairs, place_ref, xt_ref, xtp_ref, c_ref, *refs):
    ctxs, dqts, dkos, dvos, dkps, dvps = (refs[i * pairs : (i + 1) * pairs] for i in range(6))
    keep_ref, send_ref, all_ref = refs[-3:]
    samples, width, rows = xt_ref.shape
    cols = pairs * dkos[0].shape[2]
    chunk = keep_ref.shape[1]
    chunks = 2 * keep_ref.shape[0]
    per_type = chunks // 4

    def put(kind, value):
        for i in range(per_type):
            all_ref[(kind * per_type + i) ^ place_ref[0]] = value[i * chunk : (i + 1) * chunk].astype(BF16)

    xt = jnp.concatenate([xt_ref[s] for s in range(samples)], 1)
    xt_all = jnp.concatenate([xt_ref[s] for s in range(samples)] + [xtp_ref[s] for s in range(samples)], 1)

    def across(parts):
        return jnp.concatenate([jnp.concatenate([r[s] for r in parts], 0) for s in range(samples)], 1)

    def down(parts):
        return [jnp.concatenate([r[s] for r in parts], 1) for s in range(samples)]

    go = nn(across(ctxs), c_ref[...].reshape(samples * rows, width))
    put(3, jnp.concatenate([go[:, i : i + cols] for i in range(0, width, cols)], 0))
    put(0, nt(xt, across(dqts)))
    put(1, nn(xt_all, jnp.concatenate(down(dkos) + down(dkps), 0)))
    put(2, nn(xt_all, jnp.concatenate(down(dvos) + down(dvps), 0)))
    keep_ref[...] = all_ref[: chunks // 2]
    send_ref[...] = all_ref[chunks // 2 :]


def weight_grads(place, devices, xt, xtp, cotangent, parts, after):
    samples, width, rows = xt.shape
    pairs = len(parts[0])
    cols = pairs * parts[0][0].shape[1]
    half = pltpu.VMEM((devices // 2, 4 * width // devices, cols), BF16)
    whole = pl.BlockSpec(memory_space=pltpu.VMEM)
    return pl.pallas_call(
        functools.partial(weights_kernel, pairs),
        in_specs=[pl.BlockSpec(memory_space=pltpu.SMEM)] + [whole] * 3 + [whole] * (6 * pairs) + [pl.BlockSpec(memory_space=pl.ANY)] * len(after),
        out_shape=[half, half],
        scratch_shapes=[pltpu.VMEM((devices, 4 * width // devices, cols), BF16)],
        cost_estimate=cost(3),
        compiler_params=params(),
    )(place, *near(xt, xtp, cotangent), *[x for part in parts for x in part], *after)


def plan_of(levels):
    return [[0], [1]] + [list(range(low, min(low + 2, levels))) for low in range(2, levels, 2)]


def spread(number, bits):
    return sum((number >> at & 1) << bit for at, bit in enumerate(bits))


def place_of(plan):
    index = lax.axis_index("tok")
    place = jnp.int32(0)
    for bits in plan:
        digit = sum((index >> bit & 1) << at for at, bit in enumerate(bits))
        place = (place << len(bits)) + digit
    return place.reshape(1)


def exchange(x, mask):
    return lax.ppermute(x, "tok", [(i, i ^ mask) for i in range(lax.axis_size("tok"))])


def fold(kept, came, share):
    total = kept.astype(F32)
    for piece in came:
        total = total + piece.astype(F32)
    parts = [total[i : i + share].astype(BF16) for i in range(0, total.shape[0], share)]
    return parts[0], parts[1:]


def send_all(pieces, bits):
    return [exchange(piece, spread(m + 1, bits)) for m, piece in enumerate(pieces)]


def gather_all(mine, bits):
    return [mine] + [exchange(mine, spread(m, bits)) for m in range(1, 1 << len(bits))]


def tie(*values):
    return lax.optimization_barrier(values)


def spread_kernel(groups, count, place_ref, *refs):
    piece_refs, out_refs, all_ref = refs[:-5], refs[-5:-1], refs[-1]
    per_type, width = all_ref.shape[0] // 4, all_ref.shape[2]
    cols = width // groups
    for g in range(groups):
        slot = 0
        for ref in piece_refs[g * count : (g + 1) * count]:
            for i in range(ref.shape[0]):
                all_ref[slot ^ place_ref[0], :, g * cols : (g + 1) * cols] = ref[i].astype(F32)
                slot += 1
    for kind in range(3):
        out_refs[kind][...] = all_ref[kind * per_type : (kind + 1) * per_type].reshape(width, width)
    last = all_ref[3 * per_type :].reshape(groups, cols, width)
    for g in range(groups):
        for i in range(groups):
            out_refs[3][g * cols : (g + 1) * cols, i * cols : (i + 1) * cols] = last[i, :, g * cols : (g + 1) * cols]


def spread_grads(place, devices, width, pieces):
    whole = pl.BlockSpec(memory_space=pltpu.VMEM)
    groups, count = len(pieces), len(pieces[0])
    return pl.pallas_call(
        functools.partial(spread_kernel, groups, count),
        in_specs=[pl.BlockSpec(memory_space=pltpu.SMEM)] + [whole] * (groups * count),
        out_shape=[jax.ShapeDtypeStruct((width, width), F32)] * 4,
        scratch_shapes=[pltpu.VMEM((devices, 4 * width // devices, width), F32)],
        compiler_params=params(),
    )(place, *[piece for group in pieces for piece in group])


def back_kernel(groups, *refs):
    dks, dvs = refs[:groups], refs[groups : 2 * groups]
    wk_ref, wv_ref, *outs = refs[2 * groups :]
    dk = jnp.concatenate([r[0] for r in dks], 1)
    dv = jnp.concatenate([r[0] for r in dvs], 1)
    total = (nt(dk, wk_ref[...]) + nt(dv, wv_ref[...])).astype(BF16)
    sub = outs[0].shape[1]
    for i, out in enumerate(outs):
        out[0] = total[i * sub : (i + 1) * sub]


def back(dkps, dvps, w_key, w_value):
    groups = len(dkps)
    samples, rows, cols = dkps[0].shape
    width = w_key.shape[0]
    part = pl.BlockSpec((1, rows, cols), lambda s: (s, 0, 0))
    whole = pl.BlockSpec((width, width), lambda s: (0, 0))
    return pl.pallas_call(
        functools.partial(back_kernel, groups),
        grid=(samples,),
        in_specs=[part] * (2 * groups) + [whole] * 2,
        out_specs=[pl.BlockSpec((1, rows // 4, width), lambda s: (s, 0, 0))] * 4,
        out_shape=[pltpu.VMEM((samples, rows // 4, width), BF16)] * 4,
        cost_estimate=cost(1.7),
        compiler_params=params("arbitrary"),
    )(*dkps, *dvps, w_key, w_value)


def finish_kernel(groups, *refs):
    ctxs, dqts, dks, dvs = (refs[i * groups : (i + 1) * groups] for i in range(4))
    wo_ref, wq_ref, wk_ref, wv_ref, out_ref, gt_ref = refs[4 * groups :]
    ctx = jnp.concatenate([r[0] for r in ctxs], 0)
    out_ref[0] = tn(ctx, wo_ref[...]).astype(BF16)
    dqt = jnp.concatenate([r[0] for r in dqts], 0)
    dk = jnp.concatenate([r[0] for r in dks], 1)
    dv = jnp.concatenate([r[0] for r in dvs], 1)
    gt_ref[0] = tt(dqt, wq_ref[...]) + nt(dk, wk_ref[...]) + nt(dv, wv_ref[...])


def finish(ctxs, dqts, dks, dvs, w_out, w_query, w_key, w_value):
    groups = len(ctxs)
    samples, cols, rows = ctxs[0].shape
    width = w_out.shape[0]
    part = pl.BlockSpec((1, cols, rows), lambda s: (s, 0, 0))
    row_part = pl.BlockSpec((1, rows, cols), lambda s: (s, 0, 0))
    whole = pl.BlockSpec((width, width), lambda s: (0, 0))
    row_block = pl.BlockSpec((1, rows, width), lambda s: (s, 0, 0))
    return pl.pallas_call(
        functools.partial(finish_kernel, groups),
        grid=(samples,),
        in_specs=[part] * (2 * groups) + [row_part] * (2 * groups) + [whole] * 4,
        out_specs=[row_block, row_block],
        out_shape=[jax.ShapeDtypeStruct((samples, rows, width), BF16), pltpu.VMEM((samples, rows, width), F32)],
        cost_estimate=cost(4),
        compiler_params=params("arbitrary"),
    )(*ctxs, *dqts, *dks, *dvs, w_out, w_query, w_key, w_value)


def token_kernel(i0, i1, i2, i3, gt_ref, b0, b1, b2, b3, out_ref, acc_ref):
    sub = b0.shape[1]
    acc_ref[...] = gt_ref[0]
    for section, (index, came) in enumerate(((i0, b0), (i1, b1), (i2, b2), (i3, b3))):
        acc_ref[pl.ds(pl.multiple_of(index[0, section] * sub, sub), sub), :] += came[0].astype(F32)
    out_ref[0] = acc_ref[...].astype(BF16)


def token_grads(starts, partial, backs):
    samples, rows, width = partial.shape
    row_block = pl.BlockSpec((1, rows, width), lambda s: (s, 0, 0))
    came = pl.BlockSpec((1,) + backs[0].shape[1:], lambda s: (s, 0, 0))
    return pl.pallas_call(
        token_kernel,
        grid=(samples,),
        in_specs=[pl.BlockSpec(memory_space=pltpu.SMEM)] * 4 + [row_block] + [came] * 4,
        out_specs=row_block,
        out_shape=jax.ShapeDtypeStruct((samples, rows, width), BF16),
        scratch_shapes=[pltpu.VMEM((rows, width), F32)],
        compiler_params=params("arbitrary"),
    )(*starts, partial, *backs)


def pick_kernel(i0, i1, i2, i3, x_ref, o0, o1, o2, o3):
    sub = o0.shape[1]
    for section, (index, out) in enumerate(((i0, o0), (i1, o1), (i2, o2), (i3, o3))):
        out[...] = x_ref[:, pl.ds(pl.multiple_of(index[0, section] * sub, sub), sub), :]


def pick(starts, tokens):
    samples, _, width = tokens.shape
    return pl.pallas_call(
        pick_kernel,
        in_specs=[pl.BlockSpec(memory_space=pltpu.SMEM)] * 4 + [pl.BlockSpec(tokens.shape, lambda: (0, 0, 0))],
        out_shape=[pltpu.VMEM((samples, SUB, width), BF16)] * 4,
        cost_estimate=cost(1),
        compiler_params=params(),
    )(*starts, *far(tokens))


def per_device(tokens, w_query, w_key, w_value, w_out, partner_block, head_masks, cotangent):
    samples, rows, width = tokens.shape
    head_count = head_masks.shape[2]
    devices = lax.axis_size("tok")
    levels = devices.bit_length() - 1
    plan = plan_of(levels)
    place = place_of(plan)
    scale = (width // head_count) ** -0.5
    theirs = [partner(partner_block, levels - 4 + section) for section in range(4)]
    picked = pick(theirs, tokens)
    first_tokens, *picked = tie(tokens, *picked)
    arrived = [partner(piece, levels - 4 + section) for section, piece in enumerate(picked)]
    qt, ko, vo, kto, vto, dot, xt = project(first_tokens, cotangent, w_query, w_key, w_value, w_out, scale)
    e_all, *stats, vo, kto, dot = own_part(qt, ko, vto, head_count, [vo, kto, dot])
    kp, vp, ktp, vtp, xtp, e = project_partner(arrived, w_key, w_value, [e_all], [*stats, qt, vo, kto, dot])

    def run(pair, e, loads, held, after=()):
        out = attend(
            pair, head_masks[0], e, stats, qt, dot, vo, kto, (kp, vp, ktp, vtp), head_count, scale, loads, held, after
        )
        return out[:6], *out[6:]

    def weigh(parts, after=()):
        return weight_grads(place, devices, xt, xtp, cot, list(zip(*parts)), after)

    p0, e, xt = run(0, e, [e_all, xt], [xtp])
    p1, e, cot = run(1, e, [e_all, cotangent], [xtp, xt])
    first, second = [p0, p1], []
    kept0, sends0 = weigh(first)
    came = send_all([sends0], plan[0])
    p2, e = run(2, e, [e_all], [xtp, xt, cot], (sends0,))
    kept0, sends0 = fold(kept0, came, devices // 4)
    came = send_all(sends0, plan[1])
    (p3,) = run(3, e, [], [xtp, xt, cot], tuple(sends0))
    second = [p2, p3]
    kept0, _ = fold(kept0, came, devices // 4)
    kept1, sends1 = weigh(second, (kept0,))
    ctxs, dqts, dkos, dvos, dkps, dvps = zip(*(first + second))

    def scatter(kept, number):
        left = kept.shape[0] >> len(plan[number])
        sends = [kept[i : i + left] for i in range(0, kept.shape[0], left)]
        return sends[0], send_all(sends[1:], plan[number]), left

    def finish_scatter(kept):
        for number in range(3, len(plan)):
            mine, came, left = scatter(kept, number)
            kept, _ = fold(mine, came, left)
        for number in reversed(range(3, len(plan))):
            kept = jnp.concatenate(gather_all(kept, plan[number]), 0)
        return kept

    came1 = send_all([sends1], plan[0])
    mine0, came0, left = scatter(kept0, 2)
    backs = back(dkps, dvps, w_key, w_value)
    kept1, sends1 = fold(kept1, came1, devices // 4)
    came1, *backs = tie(*send_all(sends1, plan[1]), *backs)
    backs = [partner(piece, levels - 4 + i) for i, piece in enumerate(backs)]
    kept1, _ = fold(kept1, [came1], devices // 4)
    kept0, _ = fold(mine0, came0, left)
    kept0 = finish_scatter(kept0)
    mine1, *sends1 = [kept1[i : i + left] for i in range(0, kept1.shape[0], left)]
    came = send_all([jnp.concatenate([kept0, piece], 0) for piece in sends1], plan[2])
    output, partial = finish(ctxs, dqts, dkos, dvos, w_out, w_query, w_key, w_value)
    *came, partial = tie(*came, partial)
    kept1, _ = fold(mine1, [piece[left:] for piece in came], left)
    pieces0 = gather_all(jnp.concatenate([kept0] + [piece[:left] for piece in came], 0), plan[1])
    kept1 = finish_scatter(kept1)
    kept1, *backs[1:2] = tie(kept1, *backs[1:2])
    pieces1 = gather_all(kept1, plan[2])
    mine0 = jnp.concatenate(pieces0, 0)
    mine0, *backs[2:] = tie(mine0, *backs[2:])
    pieces0 = gather_all(mine0, plan[0])
    pieces1 = gather_all(jnp.concatenate(pieces1, 0), plan[1])
    mine1, *backs = tie(jnp.concatenate(pieces1, 0), *backs)
    grad_tokens = token_grads(theirs, partial, backs)
    mine1, grad_tokens = tie(mine1, grad_tokens)
    pieces1 = gather_all(mine1, plan[0])
    return (output, grad_tokens, *spread_grads(place, devices, width, [pieces0, pieces1]))


def solution(mesh):
    rows = P("groups", "tok", None)
    placed = (rows, P(), P(), P(), P(), P("tok", None), P("tok", None, None), rows)
    grads = P("groups", None)
    return jax.shard_map(
        per_device, mesh=mesh, in_specs=placed, out_specs=(rows, rows, grads, grads, grads, grads), check_vma=False
    )
```

```python
import functools

import jax
import jax.numpy as jnp
from jax import lax
from jax.experimental import pallas as pl
from jax.experimental.pallas import tpu as pltpu
from jax.sharding import PartitionSpec as P

SUB = 128
CHUNKS = ((0, 1), (2, 3))
VMEM = 14 * 1024 * 1024
F32 = jnp.float32
BF16 = jnp.bfloat16
OFF = 1e30
TILE = 128
DONE = object()


def partner(x, stride):
    return lax.ppermute(x, "tok", [(i, i ^ 1 << stride) for i in range(lax.axis_size("tok"))])


def nn(a, b):
    return lax.dot_general(a, b, (((1,), (0,)), ((), ())), preferred_element_type=F32)


def nt(a, b):
    return lax.dot_general(a, b, (((1,), (1,)), ((), ())), preferred_element_type=F32)


def tn(a, b):
    return lax.dot_general(a, b, (((0,), (0,)), ((), ())), preferred_element_type=F32)


def tt(a, b):
    return lax.dot_general(a, b, (((0,), (1,)), ((), ())), preferred_element_type=F32)


def params(*semantics):
    return pltpu.CompilerParams(vmem_limit_bytes=VMEM, dimension_semantics=semantics or None)


def cost(us):
    return pl.CostEstimate(flops=int(us * 1.1e9), bytes_accessed=int(us * 1e5), transcendentals=0)


def far(*arrays):
    return [pltpu.with_memory_space_constraint(x, pltpu.HBM) for x in arrays]


def near(*arrays):
    return [pltpu.with_memory_space_constraint(x, pltpu.VMEM) for x in arrays]


def head_rows(pair_rows, which, head_width):
    row = lax.broadcasted_iota(jnp.int32, pair_rows.shape, 0)
    keep = (row >= which * head_width) & (row < (which + 1) * head_width)
    return jnp.where(keep, pair_rows, jnp.zeros_like(pair_rows))


def project_kernel(scale, x_ref, c_ref, wq_ref, wk_ref, wv_ref, wo_ref, qt_ref, k_ref, v_ref, kt_ref, vt_ref, dot_ref, xt_ref):
    x = x_ref[0]
    xt_ref[0] = x.T
    qt_ref[0] = (tt(wq_ref[...], x).astype(BF16).astype(F32) * scale).astype(BF16)
    k = nn(x, wk_ref[...])
    v = nn(x, wv_ref[...])
    k_ref[0] = k.astype(BF16)
    v_ref[0] = v.astype(BF16)
    kt_ref[0] = k.T.astype(BF16)
    vt_ref[0] = v.T.astype(BF16)
    dot_ref[0] = nt(wo_ref[...], c_ref[0]).astype(BF16)


def project(tokens, cotangent, w_query, w_key, w_value, w_out, scale):
    samples, rows, width = tokens.shape
    row_block = pl.BlockSpec((1, rows, width), lambda s: (s, 0, 0))
    col_block = pl.BlockSpec((1, width, rows), lambda s: (s, 0, 0))
    whole = pl.BlockSpec((width, width), lambda s: (0, 0))
    by_row = pltpu.VMEM((samples, rows, width), BF16)
    by_col = pltpu.VMEM((samples, width, rows), BF16)
    far_row = pltpu.HBM((samples, rows, width), BF16)
    far_col = pltpu.HBM((samples, width, rows), BF16)
    return pl.pallas_call(
        functools.partial(project_kernel, scale),
        grid=(samples,),
        in_specs=[row_block, row_block] + [whole] * 4,
        out_specs=[col_block, row_block, row_block, col_block, col_block, col_block, col_block],
        out_shape=[by_col, by_row, far_row, far_col, by_col, far_col, far_col],
        cost_estimate=cost(5),
        compiler_params=params("arbitrary"),
    )(*far(tokens, cotangent, w_query, w_key, w_value, w_out))


def bring(sources, targets, sem):
    copies = [pltpu.make_async_copy(src, dst, sem.at[i]) for i, (src, dst) in enumerate(zip(sources, targets))]
    for copy in copies:
        copy.start()
    return copies


def project_partner_kernel(loads, x0, x1, x2, x3, wk_ref, wv_ref, *refs):
    k_ref, v_ref, kt_ref, vt_ref, xt_ref, *targets, sem = refs[-6 - loads :]
    sources = refs[:loads]
    copies = bring([sources[0].at[0], *sources[1:]], targets, sem)
    for s in range(x0.shape[0]):
        x = jnp.concatenate([x0[s], x1[s], x2[s], x3[s]], 0)
        xt_ref[s] = x.T
        k = nn(x, wk_ref[...])
        v = nn(x, wv_ref[...])
        k_ref[s] = k.astype(BF16)
        v_ref[s] = v.astype(BF16)
        kt_ref[s] = k.T.astype(BF16)
        vt_ref[s] = v.T.astype(BF16)
    for copy in copies:
        copy.wait()


def project_partner(arrived, w_key, w_value, loads, held):
    samples, sub_rows, width = arrived[0].shape
    rows = sub_rows * len(arrived)
    whole = pl.BlockSpec(memory_space=pltpu.VMEM)
    anywhere = pl.BlockSpec(memory_space=pl.ANY)
    by_row = pltpu.VMEM((samples, rows, width), BF16)
    by_col = pltpu.VMEM((samples, width, rows), BF16)
    return pl.pallas_call(
        functools.partial(project_partner_kernel, len(loads)),
        in_specs=[whole] * 6 + [anywhere] * len(loads) + [whole] * len(held),
        out_specs=[whole] * (5 + len(loads)),
        out_shape=[by_row, by_row, by_col, by_col, by_col, pltpu.VMEM(loads[0].shape[1:], BF16)]
        + [pltpu.VMEM(x.shape, x.dtype) for x in loads[1:]],
        scratch_shapes=[pltpu.SemaphoreType.DMA((len(loads),))],
        cost_estimate=cost(2.5),
        compiler_params=params(),
    )(*near(*arrived, w_key, w_value), *far(*loads), *near(*held))


def weave(*streams):
    streams = [iter(x) for x in streams]
    while streams:
        streams = [x for x in streams if next(x, DONE) is not DONE]


def down8(x, op):
    return op(x.reshape(x.shape[0] // 8, 8, x.shape[1]), axis=0)


def own_kernel(head_width, qt_ref, k_ref, vt_ref, *refs):
    loads = (len(refs) - 5) // 2
    e_ref, o_ref, st_ref, *targets, s_ref, sem = refs[loads:]
    copies = [pltpu.make_async_copy(src, dst, sem.at[i]) for i, (src, dst) in enumerate(zip(refs[:loads], targets))]

    @pl.when(pl.program_id(0) == 0)
    def _():
        for copy in copies:
            copy.start()

    samples, width, rows = qt_ref.shape
    units = [(sample, which) for sample in range(samples) for which in range(2)]

    def one_pair(pair):
        first = pl.multiple_of(pair * 2 * head_width, 2 * head_width)
        tops = {}

        def score(unit):
            sample, which = unit
            half = head_rows(qt_ref[sample, pl.ds(first, 2 * head_width), :], which, head_width)
            top = None
            for at in range(0, rows, TILE):
                s = nn(k_ref[sample, at : at + TILE, pl.ds(first, 2 * head_width)], half)
                s_ref[which, at : at + TILE, :] = s
                part = down8(s, jnp.max)
                top = part if top is None else jnp.maximum(top, part)
                yield
            tops[unit] = jnp.max(top, axis=0, keepdims=True)

        def expo(unit):
            sample, which = unit
            cols = slice(which * rows, (which + 1) * rows)
            total = None
            for at in range(0, rows, TILE):
                e = jnp.exp(s_ref[which, at : at + TILE, :] - tops[unit])
                part = down8(e, jnp.sum)
                total = part if total is None else total + part
                e_ref[0, sample, at : at + TILE, cols] = e.astype(BF16)
                yield
            total = jnp.sum(total, axis=0, keepdims=True)
            st_ref[sample, 2 * pair + which] = jnp.concatenate([tops[unit], total, jnp.zeros((6, rows), F32)], 0)

        def out(unit):
            sample, which = unit
            cols = slice(which * rows, (which + 1) * rows)
            span = pl.ds(first + which * head_width, head_width)
            o_ref[sample, 2 * pair + which] = nn(vt_ref[sample, span, :], e_ref[0, sample, :, cols])
            yield

        count = len(units)
        for i in range(count + 2):
            streams = []
            if i < count:
                streams.append(score(units[i]))
            if 1 <= i <= count:
                streams.append(expo(units[i - 1]))
            if i >= 2:
                streams.append(out(units[i - 2]))
            weave(*streams)

    one_pair(pl.program_id(0))

    @pl.when(pl.program_id(0) == pl.num_programs(0) - 1)
    def _():
        for copy in copies:
            copy.wait()


def own_part(qt, k, vt, head_count, loads):
    samples, width, rows = qt.shape
    head_width = width // head_count
    whole = pl.BlockSpec(memory_space=pltpu.VMEM)
    return pl.pallas_call(
        functools.partial(own_kernel, head_width),
        grid=(head_count // 2,),
        in_specs=[whole] * 3 + [pl.BlockSpec(memory_space=pl.ANY)] * len(loads),
        out_specs=[pl.BlockSpec((1, samples, rows, 2 * rows), lambda p: (p, 0, 0, 0))] + [whole] * (2 + len(loads)),
        out_shape=[
            pltpu.HBM((head_count // 2, samples, rows, 2 * rows), BF16),
            pltpu.VMEM((samples, head_count, head_width, rows), F32),
            pltpu.VMEM((samples, head_count, 8, rows), F32),
        ]
        + [pltpu.VMEM(x.shape, x.dtype) for x in loads],
        scratch_shapes=[pltpu.VMEM((2, rows, rows), F32), pltpu.SemaphoreType.DMA((len(loads),))],
        cost_estimate=cost(10),
        compiler_params=params("arbitrary"),
    )(*near(qt, k, vt), *far(*loads))


def attend_kernel(
    pair, head_width, scale, mask_ref, e_ref, o_ref, st_ref, qt_ref, dot_ref, vo_ref, kto_ref, kp_ref, vp_ref, ktp_ref,
    vtp_ref, *refs,
):
    s_ref, ep_ref, dsp_ref, dso_ref, ops_ref, sem = refs[-6:]
    loads = sem.shape[0]
    targets = refs[-6 - loads : -6]
    ctx_ref, dqt_ref, dko_ref, dvo_ref, dkp_ref, dvp_ref = refs[-12 - loads : -6 - loads]
    sources = [x.at[pair + 1] if len(x.shape) == 4 else x for x in refs[:loads]]
    copies = bring(sources, targets, sem)
    sections = mask_ref.shape[0]
    samples, _, rows = qt_ref.shape
    sub = kp_ref.shape[1] // sections
    both = slice(pair * 2 * head_width, (pair + 1) * 2 * head_width)
    stats = {}

    def span(which):
        return slice((2 * pair + which) * head_width, (2 * pair + which + 1) * head_width)

    def cols(which):
        return slice(which * rows, (which + 1) * rows)

    def score(unit):
        sample, which = unit
        kept = stats[unit] = {}
        kept["q"] = head_rows(qt_ref[sample, both, :], which, head_width)
        kept["g"] = head_rows(dot_ref[sample, both, :], which, head_width)
        kept["off"] = [jnp.where(mask_ref[i, 2 * pair + which] > 0, 0.0, OFF).astype(F32) for i in range(sections)]
        top = None
        for i in range(sections):
            at = slice(i * sub, (i + 1) * sub)
            s = nn(kp_ref[sample, at, both], kept["q"])
            s_ref[which, at, :] = s
            part = down8(s, jnp.max) - kept["off"][i]
            top = part if top is None else jnp.maximum(top, part)
            yield
        top_own = st_ref[sample, 2 * pair + which, 0:1, :]
        kept["top"] = jnp.maximum(top_own, jnp.max(top, axis=0, keepdims=True))
        kept["fade"] = jnp.exp(top_own - kept["top"])

    def expo(unit):
        sample, which = unit
        kept = stats[unit]
        total = None
        for i in range(sections):
            at = slice(i * sub, (i + 1) * sub)
            e = jnp.exp(s_ref[which, at, :] - (kept["top"] + kept["off"][i]))
            part = down8(e, jnp.sum)
            total = part if total is None else total + part
            ep_ref[sample, at, cols(which)] = e.astype(BF16)
            yield
        total = jnp.sum(total, axis=0, keepdims=True) + kept["fade"] * st_ref[sample, 2 * pair + which, 1:2, :]
        kept["inverse"] = 1.0 / total

    def blend(unit):
        sample, which = unit
        kept = stats[unit]
        inverse, fade = kept["inverse"], kept["fade"]
        here = slice(which * head_width, (which + 1) * head_width)
        o = fade * o_ref[sample, 2 * pair + which] + nn(vtp_ref[sample, span(which), :], ep_ref[sample, :, cols(which)])
        ctx = (o * inverse).astype(BF16)
        ctx_ref[sample, here, :] = ctx
        g = dot_ref[sample, span(which), :].astype(F32)
        kept["r"] = jnp.sum(g * ctx.astype(F32), axis=0, keepdims=True)
        q32, g32 = kept["q"].astype(F32), kept["g"].astype(F32)
        ops_ref[sample, 0, :, cols(which)] = (q32 * inverse).astype(BF16)
        ops_ref[sample, 1, :, cols(which)] = (g32 * inverse).astype(BF16)
        ops_ref[sample, 2, :, cols(which)] = (q32 * (inverse * fade)).astype(BF16)
        ops_ref[sample, 3, :, cols(which)] = (g32 * (inverse * fade)).astype(BF16)
        yield

    def slope(unit):
        sample, which = unit
        kept = stats[unit]
        for v_ref, get, put_ref in ((vp_ref, ep_ref.at[sample], dsp_ref), (vo_ref, e_ref.at[sample], dso_ref)):
            for lo in range(0, rows, TILE):
                at = slice(lo, lo + TILE)
                dp = nn(v_ref[sample, at, both], kept["g"]) - kept["r"]
                put_ref[sample, at, cols(which)] = dp.astype(BF16) * get[at, cols(which)]
                yield

    def query(unit):
        sample, which = unit
        kept = stats[unit]
        dq = nn(ktp_ref[sample, span(which), :], dsp_ref[sample, :, cols(which)])
        yield
        dq = dq + kept["fade"] * nn(kto_ref[sample, span(which), :], dso_ref[sample, :, cols(which)])
        here = slice(which * head_width, (which + 1) * head_width)
        dqt_ref[sample, here, :] = (dq * (kept["inverse"] * scale)).astype(BF16)

    def keys(sample):
        jobs = (
            (dvp_ref, ep_ref.at[sample], 1),
            (dvo_ref, e_ref.at[sample], 3),
            (dkp_ref, dsp_ref.at[sample], 0),
            (dko_ref, dso_ref.at[sample], 2),
        )
        for out_ref, left, number in jobs:
            for lo in range(0, rows, TILE):
                at = slice(lo, lo + TILE)
                out_ref[sample, at, :] = nt(left[at, :], ops_ref[sample, number]).astype(BF16)
                yield

    def chain(*streams):
        for stream in streams:
            yield from stream

    for sample in range(samples):
        one, two = (sample, 0), (sample, 1)
        before = keys(sample - 1) if sample else iter(())
        weave(score(one), before)
        weave(score(two), expo(one), before)
        weave(blend(one))
        weave(slope(one), expo(two), before)
        weave(blend(two), before)
        weave(slope(two), query(one), before)
        weave(query(two), before)
    weave(keys(samples - 1))
    for copy in copies:
        copy.wait()


def attend(pair, head_masks, e, stats, qt, dot, vo, kto, partner_rows, head_count, scale, loads, held, after):
    kp, vp, ktp, vtp = partner_rows
    samples, width, rows = qt.shape
    head_width = width // head_count
    whole = pl.BlockSpec(memory_space=pltpu.VMEM)
    anywhere = pl.BlockSpec(memory_space=pl.ANY)
    by_col = pltpu.VMEM((samples, 2 * head_width, rows), BF16)
    by_row = pltpu.VMEM((samples, rows, 2 * head_width), BF16)
    return pl.pallas_call(
        functools.partial(attend_kernel, pair, head_width, scale),
        in_specs=[pl.BlockSpec(memory_space=pltpu.SMEM)] + [whole] * 11 + [anywhere] * len(loads) + [whole] * len(held) + [anywhere] * len(after),
        out_specs=[whole] * (6 + len(loads)),
        out_shape=[by_col, by_col] + [by_row] * 4 + [pltpu.VMEM(x.shape[-4 + (x.ndim == 4) :], x.dtype) for x in loads],
        scratch_shapes=[
            pltpu.VMEM((2, rows, rows), F32),
            pltpu.VMEM((samples, rows, 2 * rows), BF16),
            pltpu.VMEM((samples, rows, 2 * rows), BF16),
            pltpu.VMEM((samples, rows, 2 * rows), BF16),
            pltpu.VMEM((samples, 4, 2 * head_width, 2 * rows), BF16),
            pltpu.SemaphoreType.DMA((max(len(loads), 1),)) if loads else pltpu.SemaphoreType.DMA((0,)),
        ],
        cost_estimate=cost(6),
        compiler_params=params(),
    )(head_masks, *near(e, *stats, qt, dot, vo, kto, kp, vp, ktp, vtp), *far(*loads), *near(*held), *after)


def weights_kernel(pairs, place_ref, xt_ref, xtp_ref, c_ref, *refs):
    ctxs, dqts, dkos, dvos, dkps, dvps = (refs[i * pairs : (i + 1) * pairs] for i in range(6))
    keep_ref, send_ref, all_ref = refs[-3:]
    samples, width, rows = xt_ref.shape
    cols = pairs * dkos[0].shape[2]
    chunk = keep_ref.shape[1]
    chunks = 2 * keep_ref.shape[0]
    per_type = chunks // 4

    def put(kind, value):
        for i in range(per_type):
            all_ref[(kind * per_type + i) ^ place_ref[0]] = value[i * chunk : (i + 1) * chunk].astype(BF16)

    xt = jnp.concatenate([xt_ref[s] for s in range(samples)], 1)
    xt_all = jnp.concatenate([xt_ref[s] for s in range(samples)] + [xtp_ref[s] for s in range(samples)], 1)

    def across(parts):
        return jnp.concatenate([jnp.concatenate([r[s] for r in parts], 0) for s in range(samples)], 1)

    def down(parts):
        return [jnp.concatenate([r[s] for r in parts], 1) for s in range(samples)]

    go = nn(across(ctxs), c_ref[...].reshape(samples * rows, width))
    put(3, jnp.concatenate([go[:, i : i + cols] for i in range(0, width, cols)], 0))
    put(0, nt(xt, across(dqts)))
    put(1, nn(xt_all, jnp.concatenate(down(dkos) + down(dkps), 0)))
    put(2, nn(xt_all, jnp.concatenate(down(dvos) + down(dvps), 0)))
    keep_ref[...] = all_ref[: chunks // 2]
    send_ref[...] = all_ref[chunks // 2 :]


def weight_grads(place, devices, xt, xtp, cotangent, parts, after):
    samples, width, rows = xt.shape
    pairs = len(parts[0])
    cols = pairs * parts[0][0].shape[1]
    half = pltpu.VMEM((devices // 2, 4 * width // devices, cols), BF16)
    whole = pl.BlockSpec(memory_space=pltpu.VMEM)
    return pl.pallas_call(
        functools.partial(weights_kernel, pairs),
        in_specs=[pl.BlockSpec(memory_space=pltpu.SMEM)] + [whole] * 3 + [whole] * (6 * pairs) + [pl.BlockSpec(memory_space=pl.ANY)] * len(after),
        out_shape=[half, half],
        scratch_shapes=[pltpu.VMEM((devices, 4 * width // devices, cols), BF16)],
        cost_estimate=cost(3),
        compiler_params=params(),
    )(place, *near(xt, xtp, cotangent), *[x for part in parts for x in part], *after)


def plan_of(levels):
    return [[0], [1]] + [list(range(low, min(low + 2, levels))) for low in range(2, levels, 2)]


def spread(number, bits):
    return sum((number >> at & 1) << bit for at, bit in enumerate(bits))


def place_of(plan):
    index = lax.axis_index("tok")
    place = jnp.int32(0)
    for bits in plan:
        digit = sum((index >> bit & 1) << at for at, bit in enumerate(bits))
        place = (place << len(bits)) + digit
    return place.reshape(1)


def exchange(x, mask):
    return lax.ppermute(x, "tok", [(i, i ^ mask) for i in range(lax.axis_size("tok"))])


def fold(kept, came, share):
    total = kept.astype(F32)
    for piece in came:
        total = total + piece.astype(F32)
    parts = [total[i : i + share].astype(BF16) for i in range(0, total.shape[0], share)]
    return parts[0], parts[1:]


def send_all(pieces, bits):
    return [exchange(piece, spread(m + 1, bits)) for m, piece in enumerate(pieces)]


def gather_all(mine, bits):
    return [mine] + [exchange(mine, spread(m, bits)) for m in range(1, 1 << len(bits))]


def tie(*values):
    return lax.optimization_barrier(values)


def spread_kernel(groups, count, place_ref, *refs):
    piece_refs, out_refs, all_ref = refs[:-5], refs[-5:-1], refs[-1]
    per_type, width = all_ref.shape[0] // 4, all_ref.shape[2]
    cols = width // groups
    for g in range(groups):
        slot = 0
        for ref in piece_refs[g * count : (g + 1) * count]:
            for i in range(ref.shape[0]):
                all_ref[slot ^ place_ref[0], :, g * cols : (g + 1) * cols] = ref[i].astype(F32)
                slot += 1
    for kind in range(3):
        out_refs[kind][...] = all_ref[kind * per_type : (kind + 1) * per_type].reshape(width, width)
    last = all_ref[3 * per_type :].reshape(groups, cols, width)
    for g in range(groups):
        for i in range(groups):
            out_refs[3][g * cols : (g + 1) * cols, i * cols : (i + 1) * cols] = last[i, :, g * cols : (g + 1) * cols]


def spread_grads(place, devices, width, pieces):
    whole = pl.BlockSpec(memory_space=pltpu.VMEM)
    groups, count = len(pieces), len(pieces[0])
    return pl.pallas_call(
        functools.partial(spread_kernel, groups, count),
        in_specs=[pl.BlockSpec(memory_space=pltpu.SMEM)] + [whole] * (groups * count),
        out_shape=[jax.ShapeDtypeStruct((width, width), F32)] * 4,
        scratch_shapes=[pltpu.VMEM((devices, 4 * width // devices, width), F32)],
        compiler_params=params(),
    )(place, *[piece for group in pieces for piece in group])


def back_kernel(groups, *refs):
    dks, dvs = refs[:groups], refs[groups : 2 * groups]
    wk_ref, wv_ref, *outs = refs[2 * groups :]
    dk = jnp.concatenate([r[0] for r in dks], 1)
    dv = jnp.concatenate([r[0] for r in dvs], 1)
    total = (nt(dk, wk_ref[...]) + nt(dv, wv_ref[...])).astype(BF16)
    sub = outs[0].shape[1]
    for i, out in enumerate(outs):
        out[0] = total[i * sub : (i + 1) * sub]


def back(dkps, dvps, w_key, w_value):
    groups = len(dkps)
    samples, rows, cols = dkps[0].shape
    width = w_key.shape[0]
    part = pl.BlockSpec((1, rows, cols), lambda s: (s, 0, 0))
    whole = pl.BlockSpec((width, width), lambda s: (0, 0))
    return pl.pallas_call(
        functools.partial(back_kernel, groups),
        grid=(samples,),
        in_specs=[part] * (2 * groups) + [whole] * 2,
        out_specs=[pl.BlockSpec((1, rows // 4, width), lambda s: (s, 0, 0))] * 4,
        out_shape=[pltpu.VMEM((samples, rows // 4, width), BF16)] * 4,
        cost_estimate=cost(1.7),
        compiler_params=params("arbitrary"),
    )(*dkps, *dvps, w_key, w_value)


def finish_kernel(groups, *refs):
    ctxs, dqts, dks, dvs = (refs[i * groups : (i + 1) * groups] for i in range(4))
    wo_ref, wq_ref, wk_ref, wv_ref, out_ref, gt_ref = refs[4 * groups :]
    ctx = jnp.concatenate([r[0] for r in ctxs], 0)
    out_ref[0] = tn(ctx, wo_ref[...]).astype(BF16)
    dqt = jnp.concatenate([r[0] for r in dqts], 0)
    dk = jnp.concatenate([r[0] for r in dks], 1)
    dv = jnp.concatenate([r[0] for r in dvs], 1)
    gt_ref[0] = tt(dqt, wq_ref[...]) + nt(dk, wk_ref[...]) + nt(dv, wv_ref[...])


def finish(ctxs, dqts, dks, dvs, w_out, w_query, w_key, w_value):
    groups = len(ctxs)
    samples, cols, rows = ctxs[0].shape
    width = w_out.shape[0]
    part = pl.BlockSpec((1, cols, rows), lambda s: (s, 0, 0))
    row_part = pl.BlockSpec((1, rows, cols), lambda s: (s, 0, 0))
    whole = pl.BlockSpec((width, width), lambda s: (0, 0))
    row_block = pl.BlockSpec((1, rows, width), lambda s: (s, 0, 0))
    return pl.pallas_call(
        functools.partial(finish_kernel, groups),
        grid=(samples,),
        in_specs=[part] * (2 * groups) + [row_part] * (2 * groups) + [whole] * 4,
        out_specs=[row_block, row_block],
        out_shape=[jax.ShapeDtypeStruct((samples, rows, width), BF16), pltpu.VMEM((samples, rows, width), F32)],
        cost_estimate=cost(4),
        compiler_params=params("arbitrary"),
    )(*ctxs, *dqts, *dks, *dvs, w_out, w_query, w_key, w_value)


def token_kernel(i0, i1, i2, i3, gt_ref, b0, b1, b2, b3, out_ref, acc_ref):
    sub = b0.shape[1]
    acc_ref[...] = gt_ref[0]
    for section, (index, came) in enumerate(((i0, b0), (i1, b1), (i2, b2), (i3, b3))):
        acc_ref[pl.ds(pl.multiple_of(index[0, section] * sub, sub), sub), :] += came[0].astype(F32)
    out_ref[0] = acc_ref[...].astype(BF16)


def token_grads(starts, partial, backs):
    samples, rows, width = partial.shape
    row_block = pl.BlockSpec((1, rows, width), lambda s: (s, 0, 0))
    came = pl.BlockSpec((1,) + backs[0].shape[1:], lambda s: (s, 0, 0))
    return pl.pallas_call(
        token_kernel,
        grid=(samples,),
        in_specs=[pl.BlockSpec(memory_space=pltpu.SMEM)] * 4 + [row_block] + [came] * 4,
        out_specs=row_block,
        out_shape=jax.ShapeDtypeStruct((samples, rows, width), BF16),
        scratch_shapes=[pltpu.VMEM((rows, width), F32)],
        compiler_params=params("arbitrary"),
    )(*starts, partial, *backs)


def pick_kernel(i0, i1, i2, i3, x_ref, o0, o1, o2, o3):
    sub = o0.shape[1]
    for section, (index, out) in enumerate(((i0, o0), (i1, o1), (i2, o2), (i3, o3))):
        out[...] = x_ref[:, pl.ds(pl.multiple_of(index[0, section] * sub, sub), sub), :]


def pick(starts, tokens):
    samples, _, width = tokens.shape
    return pl.pallas_call(
        pick_kernel,
        in_specs=[pl.BlockSpec(memory_space=pltpu.SMEM)] * 4 + [pl.BlockSpec(tokens.shape, lambda: (0, 0, 0))],
        out_shape=[pltpu.VMEM((samples, SUB, width), BF16)] * 4,
        cost_estimate=cost(1),
        compiler_params=params(),
    )(*starts, *far(tokens))


def per_device(tokens, w_query, w_key, w_value, w_out, partner_block, head_masks, cotangent):
    samples, rows, width = tokens.shape
    head_count = head_masks.shape[2]
    devices = lax.axis_size("tok")
    levels = devices.bit_length() - 1
    plan = plan_of(levels)
    place = place_of(plan)
    scale = (width // head_count) ** -0.5
    theirs = [partner(partner_block, levels - 4 + section) for section in range(4)]
    picked = pick(theirs, tokens)
    first_tokens, *picked = tie(tokens, *picked)
    arrived = [partner(picked[section], levels - 4 + section) for section in (3, 2, 1, 0)][::-1]
    qt, ko, vo, kto, vto, dot, xt = project(first_tokens, cotangent, w_query, w_key, w_value, w_out, scale)
    e_all, *stats, vo, kto, dot, near_key, near_value = own_part(qt, ko, vto, head_count, [vo, kto, dot, w_key, w_value])
    kp, vp, ktp, vtp, xtp, e = project_partner(arrived, near_key, near_value, [e_all], [*stats, qt, vo, kto, dot])

    def run(pair, e, loads, held, after=()):
        out = attend(
            pair, head_masks[0], e, stats, qt, dot, vo, kto, (kp, vp, ktp, vtp), head_count, scale, loads, held, after
        )
        return out[:6], *out[6:]

    def weigh(parts, after=()):
        return weight_grads(place, devices, xt, xtp, cot, list(zip(*parts)), after)

    p0, e, xt = run(0, e, [e_all, xt], [xtp])
    p1, e, cot = run(1, e, [e_all, cotangent], [xtp, xt])
    first, second = [p0, p1], []
    kept0, sends0 = weigh(first)
    came = send_all([sends0], plan[0])
    p2, e = run(2, e, [e_all], [xtp, xt, cot], (sends0,))
    kept0, sends0 = fold(kept0, came, devices // 4)
    came = send_all(sends0, plan[1])
    (p3,) = run(3, e, [], [xtp, xt, cot], tuple(sends0))
    second = [p2, p3]
    kept0, _ = fold(kept0, came, devices // 4)
    kept1, sends1 = weigh(second, (kept0,))
    ctxs, dqts, dkos, dvos, dkps, dvps = zip(*(first + second))

    def scatter(kept, number):
        left = kept.shape[0] >> len(plan[number])
        sends = [kept[i : i + left] for i in range(0, kept.shape[0], left)]
        return sends[0], send_all(sends[1:], plan[number]), left

    def finish_scatter(kept):
        for number in range(3, len(plan)):
            mine, came, left = scatter(kept, number)
            kept, _ = fold(mine, came, left)
        for number in reversed(range(3, len(plan))):
            kept = jnp.concatenate(gather_all(kept, plan[number]), 0)
        return kept

    came1 = send_all([sends1], plan[0])
    mine0, came0, left = scatter(kept0, 2)
    backs = back(dkps, dvps, w_key, w_value)
    kept1, sends1 = fold(kept1, came1, devices // 4)
    came1, *backs = tie(*send_all(sends1, plan[1]), *backs)
    backs = [partner(piece, levels - 4 + i) for i, piece in enumerate(backs)]
    kept1, _ = fold(kept1, [came1], devices // 4)
    kept0, _ = fold(mine0, came0, left)
    kept0 = finish_scatter(kept0)
    mine1, *sends1 = [kept1[i : i + left] for i in range(0, kept1.shape[0], left)]
    came = send_all([jnp.concatenate([kept0, piece], 0) for piece in sends1], plan[2])
    output, partial = finish(ctxs, dqts, dkos, dvos, w_out, w_query, w_key, w_value)
    *came, partial = tie(*came, partial)
    kept1, _ = fold(mine1, [piece[left:] for piece in came], left)
    pieces0 = gather_all(jnp.concatenate([kept0] + [piece[:left] for piece in came], 0), plan[1])
    kept1 = finish_scatter(kept1)
    kept1, *backs[1:2] = tie(kept1, *backs[1:2])
    pieces1 = gather_all(kept1, plan[2])
    mine0 = jnp.concatenate(pieces0, 0)
    mine0, *backs[2:] = tie(mine0, *backs[2:])
    pieces0 = gather_all(mine0, plan[0])
    pieces1 = gather_all(jnp.concatenate(pieces1, 0), plan[1])
    mine1, *backs = tie(jnp.concatenate(pieces1, 0), *backs)
    grad_tokens = token_grads(theirs, partial, backs)
    pieces1 = gather_all(mine1, plan[0])
    pieces1[-1], grad_tokens = tie(pieces1[-1], grad_tokens)
    return (output, grad_tokens, *spread_grads(place, devices, width, [pieces0, pieces1]))


def solution(mesh):
    rows = P("groups", "tok", None)
    placed = (rows, P(), P(), P(), P(), P("tok", None), P("tok", None, None), rows)
    grads = P("groups", None)
    return jax.shard_map(
        per_device, mesh=mesh, in_specs=placed, out_specs=(rows, rows, grads, grads, grads, grads), check_vma=False
    )
```

```python
import functools

import jax
import jax.numpy as jnp
from jax import lax
from jax.experimental import pallas as pl
from jax.experimental.pallas import tpu as pltpu
from jax.sharding import PartitionSpec as P

SUB = 128
CHUNKS = ((0, 1), (2, 3))
VMEM = 14 * 1024 * 1024
F32 = jnp.float32
BF16 = jnp.bfloat16
OFF = 1e30
TILE = 128
DONE = object()


def partner(x, stride):
    return lax.ppermute(x, "tok", [(i, i ^ 1 << stride) for i in range(lax.axis_size("tok"))])


def nn(a, b):
    return lax.dot_general(a, b, (((1,), (0,)), ((), ())), preferred_element_type=F32)


def nt(a, b):
    return lax.dot_general(a, b, (((1,), (1,)), ((), ())), preferred_element_type=F32)


def tn(a, b):
    return lax.dot_general(a, b, (((0,), (0,)), ((), ())), preferred_element_type=F32)


def tt(a, b):
    return lax.dot_general(a, b, (((0,), (1,)), ((), ())), preferred_element_type=F32)


def params(*semantics):
    return pltpu.CompilerParams(vmem_limit_bytes=VMEM, dimension_semantics=semantics or None)


def cost(us):
    return pl.CostEstimate(flops=int(us * 1.1e9), bytes_accessed=int(us * 1e5), transcendentals=0)


def far(*arrays):
    return [pltpu.with_memory_space_constraint(x, pltpu.HBM) for x in arrays]


def near(*arrays):
    return [pltpu.with_memory_space_constraint(x, pltpu.VMEM) for x in arrays]


def head_rows(pair_rows, which, head_width):
    row = lax.broadcasted_iota(jnp.int32, pair_rows.shape, 0)
    keep = (row >= which * head_width) & (row < (which + 1) * head_width)
    return jnp.where(keep, pair_rows, jnp.zeros_like(pair_rows))


def project_kernel(scale, x_ref, c_ref, wq_ref, wk_ref, wv_ref, wo_ref, qt_ref, k_ref, v_ref, kt_ref, vt_ref, dot_ref, xt_ref):
    x = x_ref[0]
    xt_ref[0] = x.T
    qt_ref[0] = (tt(wq_ref[...], x).astype(BF16).astype(F32) * scale).astype(BF16)
    k = nn(x, wk_ref[...])
    v = nn(x, wv_ref[...])
    k_ref[0] = k.astype(BF16)
    v_ref[0] = v.astype(BF16)
    kt_ref[0] = k.T.astype(BF16)
    vt_ref[0] = v.T.astype(BF16)
    dot_ref[0] = nt(wo_ref[...], c_ref[0]).astype(BF16)


def project(tokens, cotangent, w_query, w_key, w_value, w_out, scale):
    samples, rows, width = tokens.shape
    row_block = pl.BlockSpec((1, rows, width), lambda s: (s, 0, 0))
    col_block = pl.BlockSpec((1, width, rows), lambda s: (s, 0, 0))
    whole = pl.BlockSpec((width, width), lambda s: (0, 0))
    by_row = pltpu.VMEM((samples, rows, width), BF16)
    by_col = pltpu.VMEM((samples, width, rows), BF16)
    far_row = pltpu.HBM((samples, rows, width), BF16)
    far_col = pltpu.HBM((samples, width, rows), BF16)
    return pl.pallas_call(
        functools.partial(project_kernel, scale),
        grid=(samples,),
        in_specs=[row_block, row_block] + [whole] * 4,
        out_specs=[col_block, row_block, row_block, col_block, col_block, col_block, col_block],
        out_shape=[by_col, by_row, far_row, far_col, by_col, far_col, far_col],
        cost_estimate=cost(5),
        compiler_params=params("arbitrary"),
    )(*far(tokens, cotangent, w_query, w_key, w_value, w_out))


def bring(sources, targets, sem):
    copies = [pltpu.make_async_copy(src, dst, sem.at[i]) for i, (src, dst) in enumerate(zip(sources, targets))]
    for copy in copies:
        copy.start()
    return copies


def project_partner_kernel(x0, x1, x2, x3, wk_ref, wv_ref, *refs):
    k_ref, v_ref, kt_ref, vt_ref, xt_ref = refs[-5:]
    for s in range(x0.shape[0]):
        x = jnp.concatenate([x0[s], x1[s], x2[s], x3[s]], 0)
        xt_ref[s] = x.T
        k = nn(x, wk_ref[...])
        v = nn(x, wv_ref[...])
        k_ref[s] = k.astype(BF16)
        v_ref[s] = v.astype(BF16)
        kt_ref[s] = k.T.astype(BF16)
        vt_ref[s] = v.T.astype(BF16)


def project_partner(arrived, w_key, w_value, held):
    samples, sub_rows, width = arrived[0].shape
    rows = sub_rows * len(arrived)
    whole = pl.BlockSpec(memory_space=pltpu.VMEM)
    by_row = pltpu.VMEM((samples, rows, width), BF16)
    by_col = pltpu.VMEM((samples, width, rows), BF16)
    return pl.pallas_call(
        project_partner_kernel,
        in_specs=[whole] * (6 + len(held)),
        out_specs=[whole] * 5,
        out_shape=[by_row, by_row, by_col, by_col, by_col],
        cost_estimate=cost(2.5),
        compiler_params=params(),
    )(*near(*arrived, w_key, w_value), *near(*held))


def weave(*streams):
    streams = [iter(x) for x in streams]
    while streams:
        streams = [x for x in streams if next(x, DONE) is not DONE]


def down8(x, op):
    return op(x.reshape(x.shape[0] // 8, 8, x.shape[1]), axis=0)


def own_kernel(head_width, qt_ref, k_ref, vt_ref, *refs):
    loads = (len(refs) - 8) // 2
    e_ref, e0_ref, o_ref, st_ref, *targets, s_ref, buf_ref, sem, e_sem = refs[loads:]
    copies = [pltpu.make_async_copy(src, dst, sem.at[i]) for i, (src, dst) in enumerate(zip(refs[:loads], targets))]

    @pl.when(pl.program_id(0) == 0)
    def _():
        for copy in copies:
            copy.start()

    samples, width, rows = qt_ref.shape
    units = [(sample, which) for sample in range(samples) for which in range(2)]

    def one_pair(pair, put_ref):
        first = pl.multiple_of(pair * 2 * head_width, 2 * head_width)
        tops = {}

        def score(unit):
            sample, which = unit
            half = head_rows(qt_ref[sample, pl.ds(first, 2 * head_width), :], which, head_width)
            top = None
            for at in range(0, rows, TILE):
                s = nn(k_ref[sample, at : at + TILE, pl.ds(first, 2 * head_width)], half)
                s_ref[which, at : at + TILE, :] = s
                part = down8(s, jnp.max)
                top = part if top is None else jnp.maximum(top, part)
                yield
            tops[unit] = jnp.max(top, axis=0, keepdims=True)

        def expo(unit):
            sample, which = unit
            cols = slice(which * rows, (which + 1) * rows)
            total = None
            for at in range(0, rows, TILE):
                e = jnp.exp(s_ref[which, at : at + TILE, :] - tops[unit])
                part = down8(e, jnp.sum)
                total = part if total is None else total + part
                put_ref[sample, at : at + TILE, cols] = e.astype(BF16)
                yield
            total = jnp.sum(total, axis=0, keepdims=True)
            st_ref[sample, 2 * pair + which] = jnp.concatenate([tops[unit], total, jnp.zeros((6, rows), F32)], 0)

        def out(unit):
            sample, which = unit
            cols = slice(which * rows, (which + 1) * rows)
            span = pl.ds(first + which * head_width, head_width)
            o_ref[sample, 2 * pair + which] = nn(vt_ref[sample, span, :], put_ref[sample, :, cols])
            yield

        count = len(units)
        for i in range(count + 2):
            streams = []
            if i < count:
                streams.append(score(units[i]))
            if 1 <= i <= count:
                streams.append(expo(units[i - 1]))
            if i >= 2:
                streams.append(out(units[i - 2]))
            weave(*streams)

    step = pl.program_id(0)
    away = buf_ref.shape[0]

    def move(number):
        return pltpu.make_async_copy(buf_ref.at[number], e_ref.at[number], e_sem.at[number])

    @pl.when(step < away)
    def _():
        one_pair(step + 1, buf_ref.at[step])
        move(step).start()

    @pl.when(step == away)
    def _():
        one_pair(0, e0_ref)
        for number in range(away):
            move(number).wait()
        for copy in copies:
            copy.wait()


def own_part(qt, k, vt, head_count, loads):
    samples, width, rows = qt.shape
    head_width = width // head_count
    whole = pl.BlockSpec(memory_space=pltpu.VMEM)
    return pl.pallas_call(
        functools.partial(own_kernel, head_width),
        grid=(head_count // 2,),
        in_specs=[whole] * 3 + [pl.BlockSpec(memory_space=pl.ANY)] * len(loads),
        out_specs=[pl.BlockSpec(memory_space=pl.ANY)] + [whole] * (3 + len(loads)),
        out_shape=[
            pltpu.HBM((head_count // 2 - 1, samples, rows, 2 * rows), BF16),
            pltpu.VMEM((samples, rows, 2 * rows), BF16),
            pltpu.VMEM((samples, head_count, head_width, rows), F32),
            pltpu.VMEM((samples, head_count, 8, rows), F32),
        ]
        + [pltpu.VMEM(x.shape, x.dtype) for x in loads],
        scratch_shapes=[
            pltpu.VMEM((2, rows, rows), F32),
            pltpu.VMEM((head_count // 2 - 1, samples, rows, 2 * rows), BF16),
            pltpu.SemaphoreType.DMA((len(loads),)),
            pltpu.SemaphoreType.DMA((head_count // 2 - 1,)),
        ],
        cost_estimate=cost(10),
        compiler_params=params("arbitrary"),
    )(*near(qt, k, vt), *far(*loads))


def attend_kernel(
    pair, head_width, scale, mask_ref, e_ref, o_ref, st_ref, qt_ref, dot_ref, vo_ref, kto_ref, kp_ref, vp_ref, ktp_ref,
    vtp_ref, *refs,
):
    s_ref, ep_ref, dsp_ref, dso_ref, ops_ref, sem = refs[-6:]
    loads = sem.shape[0]
    targets = refs[-6 - loads : -6]
    ctx_ref, dqt_ref, dko_ref, dvo_ref, dkp_ref, dvp_ref = refs[-12 - loads : -6 - loads]
    sources = [x.at[pair] if len(x.shape) == 4 else x for x in refs[:loads]]
    copies = bring(sources, targets, sem)
    sections = mask_ref.shape[0]
    samples, _, rows = qt_ref.shape
    sub = kp_ref.shape[1] // sections
    both = slice(pair * 2 * head_width, (pair + 1) * 2 * head_width)
    stats = {}

    def span(which):
        return slice((2 * pair + which) * head_width, (2 * pair + which + 1) * head_width)

    def cols(which):
        return slice(which * rows, (which + 1) * rows)

    def score(unit):
        sample, which = unit
        kept = stats[unit] = {}
        kept["q"] = head_rows(qt_ref[sample, both, :], which, head_width)
        kept["g"] = head_rows(dot_ref[sample, both, :], which, head_width)
        kept["off"] = [jnp.where(mask_ref[i, 2 * pair + which] > 0, 0.0, OFF).astype(F32) for i in range(sections)]
        top = None
        for i in range(sections):
            at = slice(i * sub, (i + 1) * sub)
            s = nn(kp_ref[sample, at, both], kept["q"])
            s_ref[which, at, :] = s
            part = down8(s, jnp.max) - kept["off"][i]
            top = part if top is None else jnp.maximum(top, part)
            yield
        top_own = st_ref[sample, 2 * pair + which, 0:1, :]
        kept["top"] = jnp.maximum(top_own, jnp.max(top, axis=0, keepdims=True))
        kept["fade"] = jnp.exp(top_own - kept["top"])

    def expo(unit):
        sample, which = unit
        kept = stats[unit]
        total = None
        for i in range(sections):
            at = slice(i * sub, (i + 1) * sub)
            e = jnp.exp(s_ref[which, at, :] - (kept["top"] + kept["off"][i]))
            part = down8(e, jnp.sum)
            total = part if total is None else total + part
            ep_ref[sample, at, cols(which)] = e.astype(BF16)
            yield
        total = jnp.sum(total, axis=0, keepdims=True) + kept["fade"] * st_ref[sample, 2 * pair + which, 1:2, :]
        kept["inverse"] = 1.0 / total

    def blend(unit):
        sample, which = unit
        kept = stats[unit]
        inverse, fade = kept["inverse"], kept["fade"]
        here = slice(which * head_width, (which + 1) * head_width)
        o = fade * o_ref[sample, 2 * pair + which] + nn(vtp_ref[sample, span(which), :], ep_ref[sample, :, cols(which)])
        ctx = (o * inverse).astype(BF16)
        ctx_ref[sample, here, :] = ctx
        g = dot_ref[sample, span(which), :].astype(F32)
        kept["r"] = jnp.sum(g * ctx.astype(F32), axis=0, keepdims=True)
        q32, g32 = kept["q"].astype(F32), kept["g"].astype(F32)
        ops_ref[sample, 0, :, cols(which)] = (q32 * inverse).astype(BF16)
        ops_ref[sample, 1, :, cols(which)] = (g32 * inverse).astype(BF16)
        ops_ref[sample, 2, :, cols(which)] = (q32 * (inverse * fade)).astype(BF16)
        ops_ref[sample, 3, :, cols(which)] = (g32 * (inverse * fade)).astype(BF16)
        yield

    def slope(unit):
        sample, which = unit
        kept = stats[unit]
        for v_ref, get, put_ref in ((vp_ref, ep_ref.at[sample], dsp_ref), (vo_ref, e_ref.at[sample], dso_ref)):
            for lo in range(0, rows, TILE):
                at = slice(lo, lo + TILE)
                dp = nn(v_ref[sample, at, both], kept["g"]) - kept["r"]
                put_ref[sample, at, cols(which)] = dp.astype(BF16) * get[at, cols(which)]
                yield

    def query(unit):
        sample, which = unit
        kept = stats[unit]
        dq = nn(ktp_ref[sample, span(which), :], dsp_ref[sample, :, cols(which)])
        yield
        dq = dq + kept["fade"] * nn(kto_ref[sample, span(which), :], dso_ref[sample, :, cols(which)])
        here = slice(which * head_width, (which + 1) * head_width)
        dqt_ref[sample, here, :] = (dq * (kept["inverse"] * scale)).astype(BF16)

    def keys(sample):
        jobs = (
            (dvp_ref, ep_ref.at[sample], 1),
            (dvo_ref, e_ref.at[sample], 3),
            (dkp_ref, dsp_ref.at[sample], 0),
            (dko_ref, dso_ref.at[sample], 2),
        )
        for out_ref, left, number in jobs:
            for lo in range(0, rows, TILE):
                at = slice(lo, lo + TILE)
                out_ref[sample, at, :] = nt(left[at, :], ops_ref[sample, number]).astype(BF16)
                yield

    def chain(*streams):
        for stream in streams:
            yield from stream

    for sample in range(samples):
        one, two = (sample, 0), (sample, 1)
        before = keys(sample - 1) if sample else iter(())
        weave(score(one), before)
        weave(score(two), expo(one), before)
        weave(blend(one))
        weave(slope(one), expo(two), before)
        weave(blend(two), before)
        weave(slope(two), query(one), before)
        weave(query(two), before)
    weave(keys(samples - 1))
    for copy in copies:
        copy.wait()


def attend(pair, head_masks, e, stats, qt, dot, vo, kto, partner_rows, head_count, scale, loads, held, after):
    kp, vp, ktp, vtp = partner_rows
    samples, width, rows = qt.shape
    head_width = width // head_count
    whole = pl.BlockSpec(memory_space=pltpu.VMEM)
    anywhere = pl.BlockSpec(memory_space=pl.ANY)
    by_col = pltpu.VMEM((samples, 2 * head_width, rows), BF16)
    by_row = pltpu.VMEM((samples, rows, 2 * head_width), BF16)
    return pl.pallas_call(
        functools.partial(attend_kernel, pair, head_width, scale),
        in_specs=[pl.BlockSpec(memory_space=pltpu.SMEM)] + [whole] * 11 + [anywhere] * len(loads) + [whole] * len(held) + [anywhere] * len(after),
        out_specs=[whole] * (6 + len(loads)),
        out_shape=[by_col, by_col] + [by_row] * 4 + [pltpu.VMEM(x.shape[-4 + (x.ndim == 4) :], x.dtype) for x in loads],
        scratch_shapes=[
            pltpu.VMEM((2, rows, rows), F32),
            pltpu.VMEM((samples, rows, 2 * rows), BF16),
            pltpu.VMEM((samples, rows, 2 * rows), BF16),
            pltpu.VMEM((samples, rows, 2 * rows), BF16),
            pltpu.VMEM((samples, 4, 2 * head_width, 2 * rows), BF16),
            pltpu.SemaphoreType.DMA((max(len(loads), 1),)) if loads else pltpu.SemaphoreType.DMA((0,)),
        ],
        cost_estimate=cost(6),
        compiler_params=params(),
    )(head_masks, *near(e, *stats, qt, dot, vo, kto, kp, vp, ktp, vtp), *far(*loads), *near(*held), *after)


def weights_kernel(pairs, place_ref, xt_ref, xtp_ref, c_ref, *refs):
    ctxs, dqts, dkos, dvos, dkps, dvps = (refs[i * pairs : (i + 1) * pairs] for i in range(6))
    keep_ref, send_ref, all_ref = refs[-3:]
    samples, width, rows = xt_ref.shape
    cols = pairs * dkos[0].shape[2]
    chunk = keep_ref.shape[1]
    chunks = 2 * keep_ref.shape[0]
    per_type = chunks // 4

    def put(kind, value):
        for i in range(per_type):
            all_ref[(kind * per_type + i) ^ place_ref[0]] = value[i * chunk : (i + 1) * chunk].astype(BF16)

    xt = jnp.concatenate([xt_ref[s] for s in range(samples)], 1)
    xt_all = jnp.concatenate([xt_ref[s] for s in range(samples)] + [xtp_ref[s] for s in range(samples)], 1)

    def across(parts):
        return jnp.concatenate([jnp.concatenate([r[s] for r in parts], 0) for s in range(samples)], 1)

    def down(parts):
        return [jnp.concatenate([r[s] for r in parts], 1) for s in range(samples)]

    go = nn(across(ctxs), c_ref[...].reshape(samples * rows, width))
    put(3, jnp.concatenate([go[:, i : i + cols] for i in range(0, width, cols)], 0))
    put(0, nt(xt, across(dqts)))
    put(1, nn(xt_all, jnp.concatenate(down(dkos) + down(dkps), 0)))
    put(2, nn(xt_all, jnp.concatenate(down(dvos) + down(dvps), 0)))
    keep_ref[...] = all_ref[: chunks // 2]
    send_ref[...] = all_ref[chunks // 2 :]


def weight_grads(place, devices, xt, xtp, cotangent, parts, after):
    samples, width, rows = xt.shape
    pairs = len(parts[0])
    cols = pairs * parts[0][0].shape[1]
    half = pltpu.VMEM((devices // 2, 4 * width // devices, cols), BF16)
    whole = pl.BlockSpec(memory_space=pltpu.VMEM)
    return pl.pallas_call(
        functools.partial(weights_kernel, pairs),
        in_specs=[pl.BlockSpec(memory_space=pltpu.SMEM)] + [whole] * 3 + [whole] * (6 * pairs) + [pl.BlockSpec(memory_space=pl.ANY)] * len(after),
        out_shape=[half, half],
        scratch_shapes=[pltpu.VMEM((devices, 4 * width // devices, cols), BF16)],
        cost_estimate=cost(3),
        compiler_params=params(),
    )(place, *near(xt, xtp, cotangent), *[x for part in parts for x in part], *after)


def plan_of(levels):
    return [[0], [1]] + [list(range(low, min(low + 2, levels))) for low in range(2, levels, 2)]


def spread(number, bits):
    return sum((number >> at & 1) << bit for at, bit in enumerate(bits))


def place_of(plan):
    index = lax.axis_index("tok")
    place = jnp.int32(0)
    for bits in plan:
        digit = sum((index >> bit & 1) << at for at, bit in enumerate(bits))
        place = (place << len(bits)) + digit
    return place.reshape(1)


def exchange(x, mask):
    return lax.ppermute(x, "tok", [(i, i ^ mask) for i in range(lax.axis_size("tok"))])


def fold(kept, came, share):
    total = kept.astype(F32)
    for piece in came:
        total = total + piece.astype(F32)
    parts = [total[i : i + share].astype(BF16) for i in range(0, total.shape[0], share)]
    return parts[0], parts[1:]


def send_all(pieces, bits):
    return [exchange(piece, spread(m + 1, bits)) for m, piece in enumerate(pieces)]


def gather_all(mine, bits):
    return [mine] + [exchange(mine, spread(m, bits)) for m in range(1, 1 << len(bits))]


def tie(*values):
    return lax.optimization_barrier(values)


def spread_kernel(groups, count, place_ref, *refs):
    piece_refs, out_refs, all_ref = refs[:-5], refs[-5:-1], refs[-1]
    per_type, width = all_ref.shape[0] // 4, all_ref.shape[2]
    cols = width // groups
    for g in range(groups):
        slot = 0
        for ref in piece_refs[g * count : (g + 1) * count]:
            for i in range(ref.shape[0]):
                all_ref[slot ^ place_ref[0], :, g * cols : (g + 1) * cols] = ref[i].astype(F32)
                slot += 1
    for kind in range(3):
        out_refs[kind][...] = all_ref[kind * per_type : (kind + 1) * per_type].reshape(width, width)
    last = all_ref[3 * per_type :].reshape(groups, cols, width)
    for g in range(groups):
        for i in range(groups):
            out_refs[3][g * cols : (g + 1) * cols, i * cols : (i + 1) * cols] = last[i, :, g * cols : (g + 1) * cols]


def spread_grads(place, devices, width, pieces):
    whole = pl.BlockSpec(memory_space=pltpu.VMEM)
    groups, count = len(pieces), len(pieces[0])
    return pl.pallas_call(
        functools.partial(spread_kernel, groups, count),
        in_specs=[pl.BlockSpec(memory_space=pltpu.SMEM)] + [whole] * (groups * count),
        out_shape=[jax.ShapeDtypeStruct((width, width), F32)] * 4,
        scratch_shapes=[pltpu.VMEM((devices, 4 * width // devices, width), F32)],
        compiler_params=params(),
    )(place, *[piece for group in pieces for piece in group])


def back_kernel(groups, *refs):
    dks, dvs = refs[:groups], refs[groups : 2 * groups]
    wk_ref, wv_ref, *outs = refs[2 * groups :]
    dk = jnp.concatenate([r[0] for r in dks], 1)
    dv = jnp.concatenate([r[0] for r in dvs], 1)
    total = (nt(dk, wk_ref[...]) + nt(dv, wv_ref[...])).astype(BF16)
    sub = outs[0].shape[1]
    for i, out in enumerate(outs):
        out[0] = total[i * sub : (i + 1) * sub]


def back(dkps, dvps, w_key, w_value):
    groups = len(dkps)
    samples, rows, cols = dkps[0].shape
    width = w_key.shape[0]
    part = pl.BlockSpec((1, rows, cols), lambda s: (s, 0, 0))
    whole = pl.BlockSpec((width, width), lambda s: (0, 0))
    return pl.pallas_call(
        functools.partial(back_kernel, groups),
        grid=(samples,),
        in_specs=[part] * (2 * groups) + [whole] * 2,
        out_specs=[pl.BlockSpec((1, rows // 4, width), lambda s: (s, 0, 0))] * 4,
        out_shape=[pltpu.VMEM((samples, rows // 4, width), BF16)] * 4,
        cost_estimate=cost(1.7),
        compiler_params=params("arbitrary"),
    )(*dkps, *dvps, w_key, w_value)


def finish_kernel(groups, *refs):
    ctxs, dqts, dks, dvs = (refs[i * groups : (i + 1) * groups] for i in range(4))
    wo_ref, wq_ref, wk_ref, wv_ref, out_ref, gt_ref = refs[4 * groups :]
    ctx = jnp.concatenate([r[0] for r in ctxs], 0)
    out_ref[0] = tn(ctx, wo_ref[...]).astype(BF16)
    dqt = jnp.concatenate([r[0] for r in dqts], 0)
    dk = jnp.concatenate([r[0] for r in dks], 1)
    dv = jnp.concatenate([r[0] for r in dvs], 1)
    gt_ref[0] = tt(dqt, wq_ref[...]) + nt(dk, wk_ref[...]) + nt(dv, wv_ref[...])


def finish(ctxs, dqts, dks, dvs, w_out, w_query, w_key, w_value):
    groups = len(ctxs)
    samples, cols, rows = ctxs[0].shape
    width = w_out.shape[0]
    part = pl.BlockSpec((1, cols, rows), lambda s: (s, 0, 0))
    row_part = pl.BlockSpec((1, rows, cols), lambda s: (s, 0, 0))
    whole = pl.BlockSpec((width, width), lambda s: (0, 0))
    row_block = pl.BlockSpec((1, rows, width), lambda s: (s, 0, 0))
    return pl.pallas_call(
        functools.partial(finish_kernel, groups),
        grid=(samples,),
        in_specs=[part] * (2 * groups) + [row_part] * (2 * groups) + [whole] * 4,
        out_specs=[row_block, row_block],
        out_shape=[jax.ShapeDtypeStruct((samples, rows, width), BF16), pltpu.VMEM((samples, rows, width), F32)],
        cost_estimate=cost(4),
        compiler_params=params("arbitrary"),
    )(*ctxs, *dqts, *dks, *dvs, w_out, w_query, w_key, w_value)


def token_kernel(i0, i1, i2, i3, gt_ref, b0, b1, b2, b3, out_ref, acc_ref):
    sub = b0.shape[1]
    acc_ref[...] = gt_ref[0]
    for section, (index, came) in enumerate(((i0, b0), (i1, b1), (i2, b2), (i3, b3))):
        acc_ref[pl.ds(pl.multiple_of(index[0, section] * sub, sub), sub), :] += came[0].astype(F32)
    out_ref[0] = acc_ref[...].astype(BF16)


def token_grads(starts, partial, backs):
    samples, rows, width = partial.shape
    row_block = pl.BlockSpec((1, rows, width), lambda s: (s, 0, 0))
    came = pl.BlockSpec((1,) + backs[0].shape[1:], lambda s: (s, 0, 0))
    return pl.pallas_call(
        token_kernel,
        grid=(samples,),
        in_specs=[pl.BlockSpec(memory_space=pltpu.SMEM)] * 4 + [row_block] + [came] * 4,
        out_specs=row_block,
        out_shape=jax.ShapeDtypeStruct((samples, rows, width), BF16),
        scratch_shapes=[pltpu.VMEM((rows, width), F32)],
        compiler_params=params("arbitrary"),
    )(*starts, partial, *backs)


def pick_kernel(i0, i1, i2, i3, x_ref, o0, o1, o2, o3):
    sub = o0.shape[1]
    for section, (index, out) in enumerate(((i0, o0), (i1, o1), (i2, o2), (i3, o3))):
        out[...] = x_ref[:, pl.ds(pl.multiple_of(index[0, section] * sub, sub), sub), :]


def pick(starts, tokens):
    samples, _, width = tokens.shape
    return pl.pallas_call(
        pick_kernel,
        in_specs=[pl.BlockSpec(memory_space=pltpu.SMEM)] * 4 + [pl.BlockSpec(tokens.shape, lambda: (0, 0, 0))],
        out_shape=[pltpu.VMEM((samples, SUB, width), BF16)] * 4,
        cost_estimate=cost(1),
        compiler_params=params(),
    )(*starts, *far(tokens))


def per_device(tokens, w_query, w_key, w_value, w_out, partner_block, head_masks, cotangent):
    samples, rows, width = tokens.shape
    head_count = head_masks.shape[2]
    devices = lax.axis_size("tok")
    levels = devices.bit_length() - 1
    plan = plan_of(levels)
    place = place_of(plan)
    scale = (width // head_count) ** -0.5
    theirs = [partner(partner_block, levels - 4 + section) for section in range(4)]
    picked = pick(theirs, tokens)
    first_tokens, *picked = tie(tokens, *picked)
    arrived = [partner(picked[section], levels - 4 + section) for section in (3, 2, 1, 0)][::-1]
    qt, ko, vo, kto, vto, dot, xt = project(first_tokens, cotangent, w_query, w_key, w_value, w_out, scale)
    e_all, e, *stats, vo, kto, dot, near_key, near_value = own_part(qt, ko, vto, head_count, [vo, kto, dot, w_key, w_value])
    kp, vp, ktp, vtp, xtp = project_partner(arrived, near_key, near_value, [e, *stats, qt, vo, kto, dot])

    def run(pair, e, loads, held, after=()):
        out = attend(
            pair, head_masks[0], e, stats, qt, dot, vo, kto, (kp, vp, ktp, vtp), head_count, scale, loads, held, after
        )
        return out[:6], *out[6:]

    def weigh(parts, after=()):
        return weight_grads(place, devices, xt, xtp, cot, list(zip(*parts)), after)

    p0, e, xt = run(0, e, [e_all, xt], [xtp])
    p1, e, cot = run(1, e, [e_all, cotangent], [xtp, xt])
    first, second = [p0, p1], []
    kept0, sends0 = weigh(first)
    came = send_all([sends0], plan[0])
    p2, e = run(2, e, [e_all], [xtp, xt, cot], (sends0,))
    kept0, sends0 = fold(kept0, came, devices // 4)
    came = send_all(sends0, plan[1])
    (p3,) = run(3, e, [], [xtp, xt, cot], tuple(sends0))
    second = [p2, p3]
    kept0, _ = fold(kept0, came, devices // 4)
    kept1, sends1 = weigh(second, (kept0,))
    ctxs, dqts, dkos, dvos, dkps, dvps = zip(*(first + second))

    def scatter(kept, number):
        left = kept.shape[0] >> len(plan[number])
        sends = [kept[i : i + left] for i in range(0, kept.shape[0], left)]
        return sends[0], send_all(sends[1:], plan[number]), left

    def finish_scatter(kept):
        for number in range(3, len(plan)):
            mine, came, left = scatter(kept, number)
            kept, _ = fold(mine, came, left)
        for number in reversed(range(3, len(plan))):
            kept = jnp.concatenate(gather_all(kept, plan[number]), 0)
        return kept

    came1 = send_all([sends1], plan[0])
    mine0, came0, left = scatter(kept0, 2)
    backs = back(dkps, dvps, w_key, w_value)
    kept1, sends1 = fold(kept1, came1, devices // 4)
    came1, *backs = tie(*send_all(sends1, plan[1]), *backs)
    backs = [partner(piece, levels - 4 + i) for i, piece in enumerate(backs)]
    kept1, _ = fold(kept1, [came1], devices // 4)
    kept0, _ = fold(mine0, came0, left)
    kept0 = finish_scatter(kept0)
    mine1, *sends1 = [kept1[i : i + left] for i in range(0, kept1.shape[0], left)]
    came = send_all([jnp.concatenate([kept0, piece], 0) for piece in sends1], plan[2])
    output, partial = finish(ctxs, dqts, dkos, dvos, w_out, w_query, w_key, w_value)
    *came, partial = tie(*came, partial)
    kept1, _ = fold(mine1, [piece[left:] for piece in came], left)
    pieces0 = gather_all(jnp.concatenate([kept0] + [piece[:left] for piece in came], 0), plan[1])
    kept1 = finish_scatter(kept1)
    kept1, *backs[1:2] = tie(kept1, *backs[1:2])
    pieces1 = gather_all(kept1, plan[2])
    mine0 = jnp.concatenate(pieces0, 0)
    pieces0 = gather_all(mine0, plan[0])
    pieces1 = gather_all(jnp.concatenate(pieces1, 0), plan[1])
    mine1, *backs = tie(jnp.concatenate(pieces1, 0), *backs)
    grad_tokens = token_grads(theirs, partial, backs)
    pieces1 = gather_all(mine1, plan[0])
    pieces1[-1], grad_tokens = tie(pieces1[-1], grad_tokens)
    return (output, grad_tokens, *spread_grads(place, devices, width, [pieces0, pieces1]))


def solution(mesh):
    rows = P("groups", "tok", None)
    placed = (rows, P(), P(), P(), P(), P("tok", None), P("tok", None, None), rows)
    grads = P("groups", None)
    return jax.shard_map(
        per_device, mesh=mesh, in_specs=placed, out_specs=(rows, rows, grads, grads, grads, grads), check_vma=False
    )
```
